512 devices in a mesh: row: 32 (over x, z_hi, core), col: 16 (over y, z_lo).
Axes of the slice: x: 4, y: 8, z: 8 (z_hi: 4, z_lo: 2; z = z_hi * 2 + z_lo), core: 2. Of those that a mesh axis runs over, the one named last changes fastest.
Arguments:
- pair_tensor: bfloat16 [512, 512, 128], P('row', 'col'), may hold values from -6 to 6
- ln_gain: bfloat16 [128], replicated, may hold values from 0.099609375 to 1.8984375
- query_weight: bfloat16 [128, 128], replicated, may hold values from -1.3203125 to 1.3203125
- key_weight: bfloat16 [128, 128], replicated, may hold values from -0.5 to 0.5
- value_weight: bfloat16 [128, 128], replicated, may hold values from -0.5 to 0.5
- gate_weight: bfloat16 [128, 128], replicated, may hold values from -0.5 to 0.5
- bias_weight: bfloat16 [128, 4], replicated, may hold values from -42.426407 to 42.426407
- out_weight: bfloat16 [128, 128], replicated, may hold values from -2.109375 to 2.109375
Outputs:
- update: bfloat16 [512, 512, 128], P('row', 'col')
- update_mirror: bfloat16 [512, 512, 128], P('row', 'col')
The draws below stay inside these ranges and needn't reach their ends.
All inputs are finite; a program needn't handle non-finite values.
Results may differ from the reference program's by a relative error of at most 0.008.
The reference program's roundings to bfloat16 on the way count: a program that leaves them out, or rounds other values in their place, can miss the bound.
Values may be sent and summed in bfloat16 or wider, within the bound.
A program may use at most 64 MiB of HBM per device.

```python
import jax
import jax.numpy as jnp
from jax import lax

C = 128
H = 4
HD = 32
N = 512


def draw_bias_weight(key, part):
    key = jax.random.fold_in(key, 7)
    sample = jax.random.truncated_normal(key, -4.0, 4.0, (C, H), jnp.float32)
    return (sample * 1.5 / C ** 0.5).astype(jnp.bfloat16)


def level_of(rng, shape, split, least, largest):
    def one(position, shards_of):
        heights = jax.random.uniform(jax.random.fold_in(jax.random.fold_in(rng, 6), position), (shards_of,), jnp.float32, least / len(split), largest / len(split))
        return jnp.repeat(jnp.exp(heights), shape[position] // shards_of).reshape((-1,) + (1,) * (len(shape) - position - 1))

    level = one(*split[0])
    for cut in split[1:]:
        level = level * one(*cut)
    return level


def gaussian(stream_key, dims, scale, bound, cuts=(), held_as=jnp.bfloat16):
    array = scale * jax.random.normal(stream_key, dims, jnp.float32)
    if cuts:
        array = array * level_of(stream_key, dims, cuts, -0.22, 0.18)
    return jnp.clip(array, -bound, bound).astype(held_as)


def setup_inputs(seed: int = 0) -> dict:
    seeds = jax.random.split(jax.random.key(seed), 9)
    return {
        "pair_tensor": gaussian(seeds[0], (N, N, C), 1.0, 6.0, ((0, 32), (1, 16))),
        "ln_gain": jnp.clip(1.0 + 0.18 * jax.random.normal(seeds[1], (C,), jnp.float32), 0.099609375, 1.8984375).astype(jnp.bfloat16),
        "query_weight": gaussian(seeds[2], (C, C), (2.5 / C ** 0.5), 1.3203125),
        "key_weight": gaussian(seeds[3], (C, C), C ** -0.5, 0.5),
        "value_weight": gaussian(seeds[4], (C, C), C ** -0.5, 0.5),
        "gate_weight": gaussian(seeds[5], (C, C), C ** -0.5, 0.5),
        "bias_weight": draw_bias_weight(jax.random.fold_in(seeds[8], 71), 0),
        "out_weight": gaussian(seeds[7], (C, C), (4.0 / C ** 0.5), 2.109375),
    }


EPSILON = 1e-05

def reference(pair_tensor, ln_gain, query_weight, key_weight, value_weight, gate_weight, bias_weight, out_weight):
    entries = pair_tensor.astype(jnp.float32)
    center = lax.optimization_barrier(jnp.mean(entries, axis=-1, keepdims=True))
    spread = lax.optimization_barrier(jnp.mean(jnp.square(entries - center), axis=-1, keepdims=True))
    normed = ((entries - center) * lax.rsqrt(spread + EPSILON) * ln_gain.astype(jnp.float32)).astype(jnp.bfloat16)
    flat_rows = normed.reshape(N * N, C)
    queries = (jnp.dot(flat_rows, query_weight, preferred_element_type=jnp.float32) * HD ** (-0.5)).astype(jnp.bfloat16).reshape(N, N, H, HD)
    key_rows = jnp.dot(flat_rows, key_weight, preferred_element_type=jnp.float32).astype(jnp.bfloat16).reshape(N, N, H, HD)
    value_rows = jnp.dot(flat_rows, value_weight, preferred_element_type=jnp.float32).astype(jnp.bfloat16).reshape(N, N, H, HD)
    gating = jax.nn.sigmoid(jnp.dot(flat_rows, gate_weight, preferred_element_type=jnp.float32)).reshape(N, N, C)
    bias_full = jnp.dot(flat_rows, bias_weight, preferred_element_type=jnp.float32).astype(jnp.bfloat16)
    bias_full = bias_full.reshape(N, N, H).transpose(2, 0, 1).astype(jnp.float32)

    def one_row(inputs):
        query_row, key_row, value_row = inputs
        scores = jnp.einsum('jhd,khd->hjk', query_row.astype(jnp.float32), key_row.astype(jnp.float32)) + bias_full
        row_max = lax.optimization_barrier(jnp.max(scores, axis=-1, keepdims=True))
        exponent = jnp.exp(scores - row_max)
        denominator = lax.optimization_barrier(jnp.sum(exponent, axis=-1))
        weights = lax.optimization_barrier(exponent.astype(jnp.bfloat16)).astype(jnp.float32)
        mixed = jnp.einsum('hjk,khd->jhd', weights, value_row.astype(jnp.float32))
        mixed = mixed / denominator.T[:, :, None]
        return mixed.reshape(N, C)
    attended = lax.map(one_row, (queries, key_rows, value_rows))
    gated = (gating * attended).astype(jnp.bfloat16)
    update = jnp.dot(gated.reshape(N * N, C), out_weight, preferred_element_type=jnp.float32).astype(jnp.bfloat16).reshape(N, N, C)
    return (update, jnp.swapaxes(update, 0, 1))
```

```python
import jax
import jax.numpy as jnp
from jax import lax
from jax.experimental import pallas as pl
from jax.experimental.pallas import tpu as pltpu
from jax.sharding import PartitionSpec as P

EPSILON = 1e-05
MESH = pl.DeviceIdType.MESH
NT = (((1,), (1,)), ((), ()))


def dot(a, b):
    return jnp.dot(a, b, preferred_element_type=jnp.float32)


def dot_nt(a, b):
    return lax.dot_general(a, b, NT, preferred_element_type=jnp.float32)


def kernel(
    pair_ref,
    gain_ref,
    wq_ref,
    wk_ref,
    wv_ref,
    wg_ref,
    bw_ref,
    wo_ref,
    upd_ref,
    mir_ref,
    nrm,
    xcat,
    wbd,
    b1buf,
    bbuf,
    biasf,
    xall,
    kbuf,
    vbuf,
    qbuf,
    gbuf,
    xq,
    ustage,
    ufull,
    mstage,
    mflat,
    s1_s,
    s1_r,
    s2_s,
    s2_r,
    b1_s,
    b1_r,
    b2_s,
    b2_r,
    b3_s,
    b3_r,
    o1_s,
    o1_r,
    o2_s,
    o2_r,
    m_s,
    m_r,
):
    r = lax.axis_index("row")
    c = lax.axis_index("col")
    x = r // 8
    zh = (r // 2) % 4
    core = r % 2
    y = c // 2
    zl = c % 2
    z = zh * 2 + zl
    sibling = (r + 1 - 2 * core, c)

    def col_peer(k):
        return (r, (c + k) % 16)

    def x_row(xx):
        return xx * 8 + zh * 2 + core

    def y_peer(k):
        return (r, ((y + k) % 8) * 2 + zl)

    def z_peer(k):
        zz = (z + k) % 8
        return (x * 8 + (zz // 2) * 2 + core, y * 2 + zz % 2)

    def send(src, dst, s_sem, r_sem, dev):
        pltpu.make_async_remote_copy(
            src_ref=src,
            dst_ref=dst,
            send_sem=s_sem,
            recv_sem=r_sem,
            device_id=dev,
            device_id_type=MESH,
        ).start()

    def arrived(ref, sem):
        pltpu.make_async_copy(ref, ref, sem).wait()

    def loop(low, high, body):
        def step(k, carry):
            body(k)
            return carry

        lax.fori_loop(low, high, step, 0)

    barrier = pltpu.get_barrier_semaphore()

    def greet(dev):
        pl.semaphore_signal(barrier, inc=1, device_id=dev, device_id_type=MESH)

    loop(1, 16, lambda k: greet(col_peer(k)))
    loop(1, 8, lambda k: greet(z_peer(k)))
    loop(1, 4, lambda k: greet((x_row((x + k) % 4), c)))
    greet(sibling)

    entries = pair_ref[...].reshape(512, 128).astype(jnp.float32)
    center = jnp.mean(entries, axis=-1, keepdims=True)
    shifted = entries - center
    spread = jnp.mean(shifted * shifted, axis=-1, keepdims=True)
    gain = gain_ref[...].astype(jnp.float32)
    normed = (shifted * lax.rsqrt(spread + EPSILON) * gain).astype(jnp.bfloat16)
    nrm[...] = normed.reshape(16, 32, 128)

    xcat[...] = jnp.zeros_like(xcat)
    place = pl.multiple_of((y % 4) * 32, 32)
    for j in range(16):
        xcat[pl.ds(place, 32), j * 128 : (j + 1) * 128] = nrm[j]
    heads = lax.broadcasted_iota(jnp.int32, (64, 4), 0) // 16
    pick = heads == lax.broadcasted_iota(jnp.int32, (64, 4), 1)
    spread_w = dot_nt(pick.astype(jnp.float32).astype(jnp.bfloat16), bw_ref[...])
    row_j = lax.broadcasted_iota(jnp.int32, (64, 128), 0) % 16
    for j in range(16):
        wbd[:, j * 128 : (j + 1) * 128] = jnp.where(row_j == j, spread_w, 0.0).astype(
            jnp.bfloat16
        )
    b1buf[y] = dot_nt(wbd[...], xcat[...]).astype(jnp.bfloat16)

    pl.semaphore_wait(barrier, 26)

    loop(
        1,
        8,
        lambda k: send(b1buf.at[y], b1buf.at[y], b1_s.at[k], b1_r.at[k], y_peer(k)),
    )
    own_slot = pl.multiple_of((zl * 8 + y) * 32, 32)
    loop(
        1,
        16,
        lambda k: send(
            nrm.at[(c + k) % 16],
            xall.at[0, pl.ds(own_slot, 32)],
            s1_s.at[k],
            s1_r.at[k],
            col_peer(k),
        ),
    )
    xall[0, pl.ds(own_slot, 32)] = nrm[c]

    loop(1, 8, lambda k: arrived(b1buf.at[0], b1_r.at[k]))
    for g in range(2):
        merged = b1buf[4 * g].astype(jnp.float32)
        for i in range(1, 4):
            merged = merged + b1buf[4 * g + i].astype(jnp.float32)
        bbuf[core, z, :, g * 128 : (g + 1) * 128] = merged.astype(jnp.bfloat16)
    own_bias = bbuf.at[core, z]
    loop(1, 8, lambda k: send(own_bias, own_bias, b2_s.at[k], b2_r.at[k], z_peer(k)))
    send(own_bias, own_bias, b3_s.at[0], b3_r.at[0], sibling)

    loop(1, 16, lambda k: arrived(xall.at[0, pl.ds(0, 32)], s1_r.at[k]))
    loop(
        1,
        4,
        lambda d: send(
            xall.at[0], xall.at[d], s2_s.at[d], s2_r.at[d], (x_row((x + d) % 4), c)
        ),
    )

    def project(d):
        keys = xall[d]
        kbuf[d] = dot(keys, wk_ref[...]).astype(jnp.bfloat16)
        vbuf[d] = dot(keys, wv_ref[...]).astype(jnp.bfloat16)
        for q in range(4):
            slot = pl.multiple_of(((q % 2) * 8 + 2 * x + q // 2) * 32, 32)
            xq[q * 32 : (q + 1) * 32] = xall[d, pl.ds(slot, 32)]
        own = xq[...]
        qbuf[d] = (dot(own, wq_ref[...]) * 32**-0.5).astype(jnp.bfloat16)
        gbuf[d] = jax.nn.sigmoid(dot(own, wg_ref[...]))

    project(0)

    def forward(k):
        zz = (z - k + 8) % 8
        block = bbuf.at[core, zz]
        arrived(block, b2_r.at[k])
        send(block, block, b3_s.at[k], b3_r.at[k], sibling)

    loop(1, 8, forward)

    def next_row(d):
        arrived(xall.at[d], s2_r.at[d])
        project(d)

    loop(1, 4, next_row)

    loop(0, 8, lambda k: arrived(bbuf.at[0, 0], b3_r.at[k]))
    for half in range(2):
        for zz in range(8):
            j0 = ((zz // 2) * 2 + half) * 16
            k0 = (zz % 2) * 256
            block = bbuf[half, zz].astype(jnp.float32)
            for h in range(4):
                biasf[h, j0 : j0 + 16, k0 : k0 + 256] = block[h * 16 : (h + 1) * 16]

    head_of_lane = lax.broadcasted_iota(jnp.int32, (128, 128), 1) // 32

    def attend(d):
        queries = qbuf[d].astype(jnp.float32)
        attended = jnp.zeros((128, 128), jnp.float32)
        for h in range(4):
            mine = jnp.where(head_of_lane == h, queries, 0.0).astype(jnp.bfloat16)
            scores = dot_nt(mine, kbuf[d]) + biasf[h]
            exponent = jnp.exp(scores - jnp.max(scores, axis=-1, keepdims=True))
            denominator = jnp.sum(exponent, axis=-1, keepdims=True)
            mixed = dot(exponent.astype(jnp.bfloat16), vbuf[d])
            attended = jnp.where(head_of_lane == h, mixed / denominator, attended)
        gated = (gbuf[d] * attended).astype(jnp.bfloat16)
        ustage[d] = dot(gated, wo_ref[...]).astype(jnp.bfloat16)

    def mirror_copy(d, t):
        x_i = (x - d + 4) % 4
        to_row = x * 8 + t
        to_col = x_i * 4 + zh
        src = ustage.at[d, pl.ds(pl.multiple_of(t * 16, 16), 16)]
        dst = mstage.at[core * 16 + c]
        r_sem = m_r.at[core * 16 + c]
        here = jnp.logical_and(to_row == r, to_col == c)
        s_sem = m_s.at[d * 8 + t]
        return src, dst, s_sem, r_sem, (to_row, to_col), here

    def emit(d):
        attend(d)
        x_i = (x - d + 4) % 4

        @pl.when(d > 0)
        def _():
            send(ustage.at[d], ufull.at[x], o1_s.at[d], o1_r.at[d], (x_row(x_i), c))

        def one(t):
            src, dst, s_sem, r_sem, dev, here = mirror_copy(d, t)

            @pl.when(here)
            def _():
                pltpu.make_async_copy(src, dst, r_sem).start()

            @pl.when(jnp.logical_not(here))
            def _():
                send(src, dst, s_sem, r_sem, dev)

        loop(0, 8, one)

    loop(0, 4, emit)
    ufull[x] = ustage[0]

    loop(1, 4, lambda d: arrived(ufull.at[0], o1_r.at[d]))

    def give(k):
        cc = (c + k) % 16
        rows = pl.ds(pl.multiple_of((cc % 4) * 32, 32), 32)
        send(
            ufull.at[cc // 4, rows], upd_ref.at[c], o2_s.at[k], o2_r.at[k], col_peer(k)
        )

    loop(1, 16, give)
    upd_ref[c] = ufull[c // 4, pl.ds(pl.multiple_of((c % 4) * 32, 32), 32)]

    loop(1, 8, lambda k: arrived(b1buf.at[0], b1_s.at[k]))
    loop(1, 16, lambda k: arrived(nrm.at[0], s1_s.at[k]))
    loop(1, 8, lambda k: arrived(bbuf.at[0, 0], b2_s.at[k]))
    loop(0, 8, lambda k: arrived(bbuf.at[0, 0], b3_s.at[k]))
    loop(1, 4, lambda d: arrived(xall.at[0], s2_s.at[d]))
    loop(1, 4, lambda d: arrived(ustage.at[0], o1_s.at[d]))

    loop(0, 32, lambda k: arrived(mstage.at[0], m_r.at[k]))
    mflat[...] = mstage[...].astype(jnp.float32).reshape(512, 128)
    for j in range(16):
        mir_ref[j] = mflat[pl.ds(j, 32, stride=16), :].astype(jnp.bfloat16)

    def mirror_left(d):
        def one(t):
            src, dst, s_sem, r_sem, dev, here = mirror_copy(d, t)

            @pl.when(jnp.logical_not(here))
            def _():
                arrived(src, s_sem)

        loop(0, 8, one)

    loop(0, 4, mirror_left)
    loop(1, 16, lambda k: arrived(upd_ref.at[0], o2_r.at[k]))
    loop(1, 16, lambda k: arrived(upd_ref.at[0], o2_s.at[k]))


def per_device(pair, gain, wq, wk, wv, wg, bw, wo):
    bf16, f32 = jnp.bfloat16, jnp.float32
    vmem = pl.BlockSpec(memory_space=pltpu.VMEM)
    dma = pltpu.SemaphoreType.DMA
    tile = jax.ShapeDtypeStruct(pair.shape, bf16)
    return pl.pallas_call(
        kernel,
        out_shape=(tile, tile),
        in_specs=[vmem] * 8,
        out_specs=(vmem, vmem),
        scratch_shapes=[
            pltpu.VMEM((16, 32, 128), bf16),
            pltpu.VMEM((128, 2048), bf16),
            pltpu.VMEM((64, 2048), bf16),
            pltpu.VMEM((8, 64, 128), bf16),
            pltpu.VMEM((2, 8, 64, 256), bf16),
            pltpu.VMEM((4, 128, 512), f32),
            pltpu.VMEM((4, 512, 128), bf16),
            pltpu.VMEM((4, 512, 128), bf16),
            pltpu.VMEM((4, 512, 128), bf16),
            pltpu.VMEM((4, 128, 128), bf16),
            pltpu.VMEM((4, 128, 128), f32),
            pltpu.VMEM((128, 128), bf16),
            pltpu.VMEM((4, 128, 128), bf16),
            pltpu.VMEM((4, 128, 128), bf16),
            pltpu.VMEM((32, 16, 128), bf16),
            pltpu.VMEM((512, 128), f32),
            dma((16,)),
            dma((16,)),
            dma((4,)),
            dma((4,)),
            dma((8,)),
            dma((8,)),
            dma((8,)),
            dma((8,)),
            dma((8,)),
            dma((8,)),
            dma((4,)),
            dma((4,)),
            dma((16,)),
            dma((16,)),
            dma((32,)),
            dma((32,)),
        ],
        compiler_params=pltpu.CompilerParams(
            collective_id=0, has_side_effects=True, vmem_limit_bytes=48 * 2**20
        ),
        cost_estimate=pl.CostEstimate(
            flops=1_000_000_000, bytes_accessed=1_000_000, transcendentals=1_100_000
        ),
    )(pair, gain.reshape(1, 128), wq, wk, wv, wg, bw, wo)


def solution(mesh):
    placed = (P("row", "col", None), P(), P(), P(), P(), P(), P(), P())
    return jax.shard_map(
        per_device,
        mesh=mesh,
        in_specs=placed,
        out_specs=(P("row", "col", None), P("row", "col", None)),
        check_vma=False,
    )
```

```python
import jax
import jax.numpy as jnp
from jax import lax
from jax.experimental import pallas as pl
from jax.experimental.pallas import tpu as pltpu
from jax.sharding import PartitionSpec as P

EPSILON = 1e-05
MESH = pl.DeviceIdType.MESH
NT = (((1,), (1,)), ((), ()))


def dot(a, b):
    return jnp.dot(a, b, preferred_element_type=jnp.float32)


def dot_nt(a, b):
    return lax.dot_general(a, b, NT, preferred_element_type=jnp.float32)


def kernel(
    pair_hbm,
    gain_hbm,
    wq_hbm,
    wk_hbm,
    wv_hbm,
    wg_hbm,
    bw_hbm,
    wo_hbm,
    upd_ref,
    mir_ref,
    pair_ref,
    gain_ref,
    wq_ref,
    wk_ref,
    wv_ref,
    wg_ref,
    bw_ref,
    wo_ref,
    in_sem,
    nrm,
    xcat,
    wbd,
    b1buf,
    bbuf,
    biasf,
    xall,
    kbuf,
    vbuf,
    qbuf,
    gbuf,
    xq,
    ustage,
    ufull,
    mstage,
    mflat,
    mturn,
    s1_s,
    s1_r,
    s2_s,
    s2_r,
    b1_s,
    b1_r,
    b2_s,
    b2_r,
    b3_s,
    b3_r,
    o1_s,
    o1_r,
    o2_s,
    o2_r,
    m_s,
    m_r,
):
    r = lax.axis_index("row")
    c = lax.axis_index("col")
    x = r // 8
    zh = (r // 2) % 4
    core = r % 2
    y = c // 2
    zl = c % 2
    z = zh * 2 + zl
    sibling = (r + 1 - 2 * core, c)

    def col_peer(k):
        return (r, (c + k) % 16)

    def x_row(xx):
        return xx * 8 + zh * 2 + core

    def y_peer(k):
        return (r, ((y + k) % 8) * 2 + zl)

    def z_peer(k):
        zz = (z + k) % 8
        return (x * 8 + (zz // 2) * 2 + core, y * 2 + zz % 2)

    def send(src, dst, s_sem, r_sem, dev):
        pltpu.make_async_remote_copy(
            src_ref=src,
            dst_ref=dst,
            send_sem=s_sem,
            recv_sem=r_sem,
            device_id=dev,
            device_id_type=MESH,
        ).start()

    def arrived(ref, sem):
        pltpu.make_async_copy(ref, ref, sem).wait()

    def loop(low, high, body):
        def step(k, carry):
            body(k)
            return carry

        lax.fori_loop(low, high, step, 0)

    loads = [
        pltpu.make_async_copy(src, dst, in_sem.at[i])
        for i, (src, dst) in enumerate(
            (
                (pair_hbm, pair_ref),
                (gain_hbm, gain_ref),
                (bw_hbm, bw_ref),
                (wk_hbm, wk_ref),
                (wv_hbm, wv_ref),
                (wq_hbm, wq_ref),
                (wg_hbm, wg_ref),
                (wo_hbm, wo_ref),
            )
        )
    ]
    for load in loads:
        load.start()

    barrier = pltpu.get_barrier_semaphore()

    def greet(dev):
        pl.semaphore_signal(barrier, inc=1, device_id=dev, device_id_type=MESH)

    loop(1, 16, lambda k: greet(col_peer(k)))
    loop(1, 8, lambda k: greet(z_peer(k)))
    loop(1, 4, lambda k: greet((x_row((x + k) % 4), c)))
    greet(sibling)

    loads[0].wait()
    loads[1].wait()
    entries = pair_ref[...].reshape(512, 128).astype(jnp.float32)
    center = jnp.mean(entries, axis=-1, keepdims=True)
    shifted = entries - center
    spread = jnp.mean(shifted * shifted, axis=-1, keepdims=True)
    gain = gain_ref[...].astype(jnp.float32)
    normed = (shifted * lax.rsqrt(spread + EPSILON) * gain).astype(jnp.bfloat16)
    nrm[...] = normed.reshape(16, 32, 128)

    xcat[...] = jnp.zeros_like(xcat)
    for j in range(16):
        xcat[0:32, j * 128 : (j + 1) * 128] = nrm[j]
    heads = lax.broadcasted_iota(jnp.int32, (64, 4), 0) // 16
    pick = heads == lax.broadcasted_iota(jnp.int32, (64, 4), 1)
    loads[2].wait()
    spread_w = dot(pick.astype(jnp.float32).astype(jnp.bfloat16), bw_ref[...])
    row_j = lax.broadcasted_iota(jnp.int32, (64, 128), 0) % 16
    for j in range(16):
        wbd[:, j * 128 : (j + 1) * 128] = jnp.where(row_j == j, spread_w, 0.0).astype(
            jnp.bfloat16
        )
    by_head = dot_nt(wbd[...], xcat[...])
    packed = by_head[0:16]
    for h in range(1, 4):
        packed = packed + pltpu.roll(by_head[16 * h : 16 * h + 16], 32 * h, 1)
    b1buf[y] = packed.astype(jnp.bfloat16)

    pl.semaphore_wait(barrier, 26)

    loop(
        1,
        8,
        lambda k: send(b1buf.at[y], b1buf.at[y], b1_s.at[k], b1_r.at[k], y_peer(k)),
    )
    own_slot = pl.multiple_of((zl * 8 + y) * 32, 32)
    loop(
        1,
        16,
        lambda k: send(
            nrm.at[(c + k) % 16],
            xall.at[0, pl.ds(own_slot, 32)],
            s1_s.at[k],
            s1_r.at[k],
            col_peer(k),
        ),
    )
    xall[0, pl.ds(own_slot, 32)] = nrm[c]

    loop(1, 8, lambda k: arrived(b1buf.at[0], b1_r.at[k]))
    lane_group = lax.broadcasted_iota(jnp.int32, (16, 128), 1) // 32
    for g in range(2):
        tiles = [b1buf[4 * g + i].astype(jnp.float32) for i in range(4)]
        for h in range(4):
            merged = jnp.zeros((16, 128), jnp.float32)
            for i in range(4):
                turn = (i - h) * 32 % 128
                moved = pltpu.roll(tiles[i], turn, 1) if turn else tiles[i]
                merged = jnp.where(lane_group == i, moved, merged)
            bbuf[core, z, h * 16 : (h + 1) * 16, g * 128 : (g + 1) * 128] = merged.astype(
                jnp.bfloat16
            )
    own_bias = bbuf.at[core, z]
    loop(1, 8, lambda k: send(own_bias, own_bias, b2_s.at[k], b2_r.at[k], z_peer(k)))
    send(own_bias, own_bias, b3_s.at[0], b3_r.at[0], sibling)

    loop(1, 16, lambda k: arrived(xall.at[0, pl.ds(0, 32)], s1_r.at[k]))
    loop(
        1,
        4,
        lambda d: send(
            xall.at[0], xall.at[d], s2_s.at[d], s2_r.at[d], (x_row((x + d) % 4), c)
        ),
    )

    def project(d):
        keys = xall[d]
        kbuf[d] = dot(keys, wk_ref[...]).astype(jnp.bfloat16)
        vbuf[d] = dot(keys, wv_ref[...]).astype(jnp.bfloat16)
        for q in range(4):
            slot = pl.multiple_of(((q % 2) * 8 + 2 * x + q // 2) * 32, 32)
            xq[q * 32 : (q + 1) * 32] = xall[d, pl.ds(slot, 32)]
        own = xq[...]
        qbuf[d] = (dot(own, wq_ref[...]) * 32**-0.5).astype(jnp.bfloat16)
        gbuf[d] = jax.nn.sigmoid(dot(own, wg_ref[...]))

    for load in loads[3:]:
        load.wait()
    project(0)

    def forward(k):
        zz = (z - k + 8) % 8
        block = bbuf.at[core, zz]
        arrived(block, b2_r.at[k])
        send(block, block, b3_s.at[k], b3_r.at[k], sibling)

    loop(1, 8, forward)

    def next_row(d):
        arrived(xall.at[d], s2_r.at[d])
        project(d)

    loop(1, 4, next_row)

    loop(0, 8, lambda k: arrived(bbuf.at[0, 0], b3_r.at[k]))
    for half in range(2):
        for zz in range(8):
            j0 = ((zz // 2) * 2 + half) * 16
            k0 = (zz % 2) * 256
            block = bbuf[half, zz].astype(jnp.float32)
            for h in range(4):
                biasf[h, j0 : j0 + 16, k0 : k0 + 256] = block[h * 16 : (h + 1) * 16]

    head_of_lane = lax.broadcasted_iota(jnp.int32, (128, 128), 1) // 32

    def attend(d):
        queries = qbuf[d].astype(jnp.float32)
        attended = jnp.zeros((128, 128), jnp.float32)
        for h in range(4):
            mine = jnp.where(head_of_lane == h, queries, 0.0).astype(jnp.bfloat16)
            scores = dot_nt(mine, kbuf[d]) + biasf[h]
            exponent = jnp.exp(scores - jnp.max(scores, axis=-1, keepdims=True))
            denominator = jnp.sum(exponent, axis=-1, keepdims=True)
            mixed = dot(exponent.astype(jnp.bfloat16), vbuf[d])
            attended = jnp.where(head_of_lane == h, mixed / denominator, attended)
        gated = (gbuf[d] * attended).astype(jnp.bfloat16)
        ustage[d] = dot(gated, wo_ref[...]).astype(jnp.bfloat16)

    def mirror_copy(d, t):
        x_i = (x - d + 4) % 4
        to_row = x * 8 + t
        to_col = x_i * 4 + zh
        src = ustage.at[d, pl.ds(pl.multiple_of(t * 16, 16), 16)]
        dst = mstage.at[core * 16 + c]
        r_sem = m_r.at[core * 16 + c]
        here = jnp.logical_and(to_row == r, to_col == c)
        s_sem = m_s.at[d * 8 + t]
        return src, dst, s_sem, r_sem, (to_row, to_col), here

    def emit(d):
        attend(d)
        x_i = (x - d + 4) % 4

        @pl.when(d > 0)
        def _():
            send(ustage.at[d], ufull.at[x], o1_s.at[d], o1_r.at[d], (x_row(x_i), c))

        def one(t):
            src, dst, s_sem, r_sem, dev, here = mirror_copy(d, t)

            @pl.when(here)
            def _():
                pltpu.make_async_copy(src, dst, r_sem).start()

            @pl.when(jnp.logical_not(here))
            def _():
                send(src, dst, s_sem, r_sem, dev)

        loop(0, 8, one)

    loop(0, 4, lambda n: emit((n + 1) % 4))
    ufull[x] = ustage[0]

    def give(group):
        def one(q):
            cc = group * 4 + q
            src = ufull.at[group, pl.ds(pl.multiple_of(q * 32, 32), 32)]
            dst = upd_ref.at[c]
            k = (cc - c + 16) % 16

            @pl.when(cc == c)
            def _():
                pltpu.make_async_copy(src, dst, o2_r.at[0]).start()

            @pl.when(cc != c)
            def _():
                send(src, dst, o2_s.at[k], o2_r.at[k], (r, cc))

        loop(0, 4, one)

    give(x)

    def pass_on(d):
        arrived(ufull.at[0], o1_r.at[d])
        give((x + d) % 4)

    loop(1, 4, pass_on)

    loop(1, 8, lambda k: arrived(b1buf.at[0], b1_s.at[k]))
    loop(1, 16, lambda k: arrived(nrm.at[0], s1_s.at[k]))
    loop(1, 8, lambda k: arrived(bbuf.at[0, 0], b2_s.at[k]))
    loop(0, 8, lambda k: arrived(bbuf.at[0, 0], b3_s.at[k]))
    loop(1, 4, lambda d: arrived(xall.at[0], s2_s.at[d]))
    loop(1, 4, lambda d: arrived(ustage.at[0], o1_s.at[d]))

    loop(0, 32, lambda k: arrived(mstage.at[0], m_r.at[k]))
    mflat[...] = mstage[...].astype(jnp.float32).reshape(512, 128)
    for j in range(16):
        mturn[j] = mflat[pl.ds(j, 32, stride=16), :].astype(jnp.bfloat16)
    own_mirror = pltpu.make_async_copy(mturn, mir_ref, o2_s.at[0])
    own_mirror.start()

    def mirror_left(d):
        def one(t):
            src, dst, s_sem, r_sem, dev, here = mirror_copy(d, t)

            @pl.when(jnp.logical_not(here))
            def _():
                arrived(src, s_sem)

        loop(0, 8, one)

    loop(0, 4, mirror_left)
    own_mirror.wait()
    loop(0, 16, lambda k: arrived(upd_ref.at[0], o2_r.at[k]))
    loop(1, 16, lambda k: arrived(upd_ref.at[0], o2_s.at[k]))


def place(upd_hbm, mir_hbm, upd_out, mir_out, upd, mir, sem):
    reads = [
        pltpu.make_async_copy(upd_hbm, upd, sem.at[0]),
        pltpu.make_async_copy(mir_hbm, mir, sem.at[1]),
    ]
    writes = [
        pltpu.make_async_copy(upd, upd_out, sem.at[0]),
        pltpu.make_async_copy(mir, mir_out, sem.at[1]),
    ]
    for read in reads:
        read.start()
    for read, write in zip(reads, writes):
        read.wait()
        write.start()
    for write in writes:
        write.wait()


def per_device(pair, gain, wq, wk, wv, wg, bw, wo):
    bf16, f32 = jnp.bfloat16, jnp.float32
    hbm = pl.BlockSpec(memory_space=pl.ANY)
    dma = pltpu.SemaphoreType.DMA
    tile = jax.ShapeDtypeStruct(pair.shape, bf16)
    update, mirrored = pl.pallas_call(
        kernel,
        out_shape=(tile, tile),
        in_specs=[hbm] * 8,
        out_specs=(hbm, hbm),
        scratch_shapes=[
            pltpu.VMEM((16, 32, 128), bf16),
            pltpu.VMEM((1, 128), bf16),
            pltpu.VMEM((128, 128), bf16),
            pltpu.VMEM((128, 128), bf16),
            pltpu.VMEM((128, 128), bf16),
            pltpu.VMEM((128, 128), bf16),
            pltpu.VMEM((4, 128), bf16),
            pltpu.VMEM((128, 128), bf16),
            dma((8,)),
            pltpu.VMEM((16, 32, 128), bf16),
            pltpu.VMEM((128, 2048), bf16),
            pltpu.VMEM((64, 2048), bf16),
            pltpu.VMEM((8, 16, 128), bf16),
            pltpu.VMEM((2, 8, 64, 256), bf16),
            pltpu.VMEM((4, 128, 512), f32),
            pltpu.VMEM((4, 512, 128), bf16),
            pltpu.VMEM((4, 512, 128), bf16),
            pltpu.VMEM((4, 512, 128), bf16),
            pltpu.VMEM((4, 128, 128), bf16),
            pltpu.VMEM((4, 128, 128), f32),
            pltpu.VMEM((128, 128), bf16),
            pltpu.VMEM((4, 128, 128), bf16),
            pltpu.VMEM((4, 128, 128), bf16),
            pltpu.VMEM((32, 16, 128), bf16),
            pltpu.VMEM((512, 128), f32),
            pltpu.VMEM((16, 32, 128), bf16),
            dma((16,)),
            dma((16,)),
            dma((4,)),
            dma((4,)),
            dma((8,)),
            dma((8,)),
            dma((8,)),
            dma((8,)),
            dma((8,)),
            dma((8,)),
            dma((4,)),
            dma((4,)),
            dma((16,)),
            dma((16,)),
            dma((32,)),
            dma((32,)),
        ],
        compiler_params=pltpu.CompilerParams(
            collective_id=0, has_side_effects=True, vmem_limit_bytes=56 * 2**20
        ),
        cost_estimate=pl.CostEstimate(
            flops=1_000_000_000, bytes_accessed=1_000_000, transcendentals=1_100_000
        ),
    )(pair, gain.reshape(1, 128), wq, wk, wv, wg, bw.T, wo)
    return pl.pallas_call(
        place,
        out_shape=(tile, tile),
        in_specs=[hbm, hbm],
        out_specs=(hbm, hbm),
        scratch_shapes=[
            pltpu.VMEM((16, 32, 128), bf16),
            pltpu.VMEM((16, 32, 128), bf16),
            dma((2,)),
        ],
        compiler_params=pltpu.CompilerParams(vmem_limit_bytes=56 * 2**20),
        cost_estimate=pl.CostEstimate(flops=0, bytes_accessed=524288, transcendentals=0),
    )(update, mirrored)


def solution(mesh):
    placed = (P("row", "col", None), P(), P(), P(), P(), P(), P(), P())
    return jax.shard_map(
        per_device,
        mesh=mesh,
        in_specs=placed,
        out_specs=(P("row", "col", None), P("row", "col", None)),
        check_vma=False,
    )
```

```python
import jax
import jax.numpy as jnp
from jax import lax
from jax.experimental import pallas as pl
from jax.experimental.pallas import tpu as pltpu
from jax.sharding import PartitionSpec as P

EPSILON = 1e-05
MESH = pl.DeviceIdType.MESH
NT = (((1,), (1,)), ((), ()))


def dot(a, b):
    return jnp.dot(a, b, preferred_element_type=jnp.float32)


def div(a, b):
    return lax.div(a, jnp.int32(b))


def rem(a, b):
    return lax.rem(a, jnp.int32(b))


def outward(n, middle):
    return middle + div(n + 1, 2) * (1 - 2 * rem(n, 2))


def dot_nt(a, b):
    return lax.dot_general(a, b, NT, preferred_element_type=jnp.float32)


def kernel(
    pair_hbm,
    gain_hbm,
    wq_hbm,
    wk_hbm,
    wv_hbm,
    wg_hbm,
    bw_hbm,
    wo_hbm,
    upd_ref,
    mir_ref,
    pair_ref,
    gain_ref,
    wq_ref,
    wk_ref,
    wv_ref,
    wg_ref,
    bw_ref,
    wo_ref,
    in_sem,
    nrm,
    xcat,
    wbd,
    b1buf,
    bbuf,
    biasf,
    xall,
    wkt,
    vbuf,
    scores,
    weights,
    inverse,
    gbuf,
    xq,
    ustage,
    ufull,
    mstage,
    mflat,
    mturn,
    s1_s,
    s1_r,
    s2_s,
    s2_r,
    b1_s,
    b1_r,
    b2_s,
    b2_r,
    b3_s,
    b3_r,
    o1_s,
    o1_r,
    o2_s,
    o2_r,
    m_s,
    m_r,
):
    r = lax.axis_index("row")
    c = lax.axis_index("col")
    x = div(r, 8)
    zh = rem(div(r, 2), 4)
    core = rem(r, 2)
    y = div(c, 2)
    zl = rem(c, 2)
    z = zh * 2 + zl
    sibling = (r + 1 - 2 * core, c)

    def col_peer(k):
        return (r, rem(c + k, 16))

    def x_row(xx):
        return xx * 8 + zh * 2 + core

    def y_peer(k):
        return (r, rem(y + k, 8) * 2 + zl)

    def z_peer(k):
        zz = rem(z + k, 8)
        return (x * 8 + div(zz, 2) * 2 + core, y * 2 + rem(zz, 2))

    def send(src, dst, s_sem, r_sem, dev):
        pltpu.make_async_remote_copy(
            src_ref=src,
            dst_ref=dst,
            send_sem=s_sem,
            recv_sem=r_sem,
            device_id=dev,
            device_id_type=MESH,
        ).start()

    def arrived(ref, sem):
        pltpu.make_async_copy(ref, ref, sem).wait()

    def loop(low, high, body):
        def step(k, carry):
            body(k)
            return carry

        lax.fori_loop(low, high, step, 0)

    loads = [
        pltpu.make_async_copy(src, dst, in_sem.at[i])
        for i, (src, dst) in enumerate(
            (
                (pair_hbm, pair_ref),
                (gain_hbm, gain_ref),
                (bw_hbm, bw_ref),
                (wk_hbm, wk_ref),
                (wv_hbm, wv_ref),
                (wq_hbm, wq_ref),
                (wg_hbm, wg_ref),
                (wo_hbm, wo_ref),
            )
        )
    ]
    loads[0].start()

    barrier = pltpu.get_barrier_semaphore()

    def greet(dev):
        pl.semaphore_signal(barrier, inc=1, device_id=dev, device_id_type=MESH)

    loop(0, 15, lambda n: greet(col_peer(outward(n, 8))))
    loop(0, 7, lambda n: greet(z_peer(outward(n, 4))))
    loop(1, 4, lambda k: greet((x_row(rem(x + k, 4)), c)))
    greet(sibling)
    for load in loads[1:]:
        load.start()

    loads[0].wait()
    loads[1].wait()
    entries = pair_ref[...].reshape(512, 128).astype(jnp.float32)
    center = jnp.mean(entries, axis=-1, keepdims=True)
    shifted = entries - center
    spread = jnp.mean(shifted * shifted, axis=-1, keepdims=True)
    gain = gain_ref[...].astype(jnp.float32)
    normed = (shifted * lax.rsqrt(spread + EPSILON) * gain).astype(jnp.bfloat16)
    nrm[...] = normed.reshape(16, 32, 128)

    xcat[...] = jnp.zeros_like(xcat)
    for j in range(16):
        xcat[0:32, j * 128 : (j + 1) * 128] = nrm[j]
    heads = lax.broadcasted_iota(jnp.int32, (64, 4), 0) // 16
    pick = heads == lax.broadcasted_iota(jnp.int32, (64, 4), 1)
    loads[2].wait()
    spread_w = dot(pick.astype(jnp.float32).astype(jnp.bfloat16), bw_ref[...])
    row_j = lax.broadcasted_iota(jnp.int32, (64, 128), 0) % 16
    for j in range(16):
        wbd[:, j * 128 : (j + 1) * 128] = jnp.where(row_j == j, spread_w, 0.0).astype(
            jnp.bfloat16
        )
    by_head = dot_nt(wbd[...], xcat[...])
    packed = by_head[0:16]
    for h in range(1, 4):
        packed = packed + pltpu.roll(by_head[16 * h : 16 * h + 16], 32 * h, 1)
    b1buf[y] = packed.astype(jnp.bfloat16)

    loads[3].wait()
    wkt[...] = wk_ref[...].astype(jnp.float32).T.astype(jnp.bfloat16)

    pl.semaphore_wait(barrier, 26)

    def send_tile(n):
        k = outward(n, 4)
        send(b1buf.at[y], b1buf.at[y], b1_s.at[k], b1_r.at[k], y_peer(k))

    loop(0, 7, send_tile)
    own_slot = pl.multiple_of((zl * 8 + y) * 32, 32)

    def send_row(n):
        k = outward(n, 8)
        send(
            nrm.at[rem(c + k, 16)],
            xall.at[0, pl.ds(own_slot, 32)],
            s1_s.at[k],
            s1_r.at[k],
            col_peer(k),
        )

    loop(0, 15, send_row)
    xall[0, pl.ds(own_slot, 32)] = nrm[c]

    loop(1, 8, lambda k: arrived(b1buf.at[0], b1_r.at[k]))
    lane_group = lax.broadcasted_iota(jnp.int32, (16, 128), 1) // 32
    for g in range(2):
        tiles = [b1buf[4 * g + i].astype(jnp.float32) for i in range(4)]
        for h in range(4):
            merged = jnp.zeros((16, 128), jnp.float32)
            for i in range(4):
                turn = (i - h) * 32 % 128
                moved = pltpu.roll(tiles[i], turn, 1) if turn else tiles[i]
                merged = jnp.where(lane_group == i, moved, merged)
            bbuf[core, z, h * 16 : (h + 1) * 16, g * 128 : (g + 1) * 128] = merged.astype(
                jnp.bfloat16
            )
    own_bias = bbuf.at[core, z]

    def send_bias(n):
        k = outward(n, 4)
        send(own_bias, own_bias, b2_s.at[k], b2_r.at[k], z_peer(k))

    loop(0, 7, send_bias)
    send(own_bias, own_bias, b3_s.at[0], b3_r.at[0], sibling)

    loop(1, 16, lambda k: arrived(xall.at[0, pl.ds(0, 32)], s1_r.at[k]))
    loop(
        1,
        4,
        lambda d: send(
            xall.at[0], xall.at[d], s2_s.at[d], s2_r.at[d], (x_row(rem(x + d, 4)), c)
        ),
    )

    def project(d):
        keys = xall[d]
        kt = dot_nt(wkt[...], keys).astype(jnp.bfloat16)
        values = dot(keys, wv_ref[...])
        for h in range(4):
            vbuf[d, h * 512 : (h + 1) * 512] = jnp.where(
                head_of_key == h, values, 0.0
            ).astype(jnp.bfloat16)
        for q in range(4):
            slot = pl.multiple_of(((q % 2) * 8 + 2 * x + q // 2) * 32, 32)
            xq[q * 32 : (q + 1) * 32] = xall[d, pl.ds(slot, 32)]
        own = xq[...]
        gbuf[d] = jax.nn.sigmoid(dot(own, wg_ref[...]))
        queries = (dot(own, wq_ref[...]) * 32**-0.5).astype(jnp.bfloat16)
        queries = queries.astype(jnp.float32)
        by_head = [
            jnp.where(head_of_lane == h, queries, 0.0).astype(jnp.bfloat16)
            for h in range(4)
        ]
        scores[d] = dot(jnp.concatenate(by_head, 0), kt)

    def lay_bias(half, zz):
        block = bbuf[half, zz].astype(jnp.float32)
        j0 = pl.multiple_of((div(zz, 2) * 2 + half) * 16, 16)
        for h in range(4):
            biasf[rem(zz, 2), h, pl.ds(j0, 16)] = block[h * 16 : (h + 1) * 16]

    head_of_lane = lax.broadcasted_iota(jnp.int32, (128, 128), 1) // 32
    head_of_key = lax.broadcasted_iota(jnp.int32, (512, 128), 1) // 32

    for load in loads[4:]:
        load.wait()
    project(0)
    lay_bias(core, z)

    def forward(n):
        k = outward(6 - n, 4)
        zz = rem(z - k + 8, 8)
        block = bbuf.at[core, zz]
        arrived(block, b2_r.at[k])
        send(block, block, b3_s.at[k], b3_r.at[k], sibling)
        lay_bias(core, zz)

    loop(0, 7, forward)

    def next_row(d):
        arrived(xall.at[d], s2_r.at[d])
        project(d)

    loop(1, 4, next_row)

    def take_bias(n):
        k = outward(7 - n, 4)
        zz = rem(z - k + 8, 8)
        arrived(bbuf.at[0, 0], b3_r.at[k])
        lay_bias(1 - core, zz)

    loop(0, 8, take_bias)

    def weigh(d):
        scale = jnp.zeros((128, 128), jnp.float32)
        for h in range(4):
            bias = jnp.concatenate([biasf[0, h], biasf[1, h]], 1)
            logits = scores[d, h * 128 : (h + 1) * 128] + bias
            exponent = jnp.exp(logits - jnp.max(logits, axis=-1, keepdims=True))
            denominator = jnp.sum(exponent, axis=-1, keepdims=True)
            weights[d, :, h * 512 : (h + 1) * 512] = exponent.astype(jnp.bfloat16)
            scale = jnp.where(head_of_lane == h, 1.0 / denominator, scale)
        inverse[d] = scale

    def mix(d):
        attended = dot(weights[d], vbuf[d]) * inverse[d]
        gated = (gbuf[d] * attended).astype(jnp.bfloat16)
        ustage[d] = dot(gated, wo_ref[...]).astype(jnp.bfloat16)

    def mirror_copy(d, t):
        x_i = rem(x - d + 4, 4)
        to_row = x * 8 + t
        to_col = x_i * 4 + zh
        src = ustage.at[d, pl.ds(pl.multiple_of(t * 16, 16), 16)]
        dst = mstage.at[core * 16 + c]
        r_sem = m_r.at[core * 16 + c]
        here = jnp.logical_and(to_row == r, to_col == c)
        s_sem = m_s.at[d * 8 + t]
        return src, dst, s_sem, r_sem, (to_row, to_col), here

    def emit(d):
        if d > 0:
            dev = (x_row(rem(x - d + 4, 4)), c)
            send(ustage.at[d], ufull.at[x], o1_s.at[d], o1_r.at[d], dev)

        def one(n):
            t = rem(zh * 2 + 4 + n, 8)
            src, dst, s_sem, r_sem, dev, here = mirror_copy(d, t)

            @pl.when(here)
            def _():
                pltpu.make_async_copy(src, dst, r_sem).start()

            @pl.when(jnp.logical_not(here))
            def _():
                send(src, dst, s_sem, r_sem, dev)

        loop(0, 8, one)

    weigh(1)
    weigh(2)
    mix(1)
    emit(1)
    weigh(3)
    mix(2)
    emit(2)
    weigh(0)
    mix(3)
    emit(3)
    mix(0)
    emit(0)
    ufull[x] = ustage[0]

    def give(group):
        def one(q):
            cc = group * 4 + q
            src = ufull.at[group, pl.ds(pl.multiple_of(q * 32, 32), 32)]
            dst = upd_ref.at[c]
            k = rem(cc - c + 16, 16)

            @pl.when(cc == c)
            def _():
                pltpu.make_async_copy(src, dst, o2_r.at[0]).start()

            @pl.when(cc != c)
            def _():
                send(src, dst, o2_s.at[k], o2_r.at[k], (r, cc))

        loop(0, 4, one)

    give(x)

    def pass_on(d):
        arrived(ufull.at[0], o1_r.at[d])
        give(rem(x + d, 4))

    loop(1, 4, pass_on)

    loop(1, 8, lambda k: arrived(b1buf.at[0], b1_s.at[k]))
    loop(1, 16, lambda k: arrived(nrm.at[0], s1_s.at[k]))
    loop(1, 8, lambda k: arrived(bbuf.at[0, 0], b2_s.at[k]))
    loop(0, 8, lambda k: arrived(bbuf.at[0, 0], b3_s.at[k]))
    loop(1, 4, lambda d: arrived(xall.at[0], s2_s.at[d]))
    loop(1, 4, lambda d: arrived(ustage.at[0], o1_s.at[d]))

    loop(0, 32, lambda k: arrived(mstage.at[0], m_r.at[k]))
    mflat[...] = mstage[...].astype(jnp.float32).reshape(512, 128)
    for j in range(16):
        mturn[j] = mflat[pl.ds(j, 32, stride=16), :].astype(jnp.bfloat16)
    own_mirror = pltpu.make_async_copy(mturn, mir_ref, o2_s.at[0])
    own_mirror.start()

    def mirror_left(d):
        def one(t):
            src, dst, s_sem, r_sem, dev, here = mirror_copy(d, t)

            @pl.when(jnp.logical_not(here))
            def _():
                arrived(src, s_sem)

        loop(0, 8, one)

    loop(0, 4, mirror_left)
    own_mirror.wait()
    loop(0, 16, lambda k: arrived(upd_ref.at[0], o2_r.at[k]))
    loop(1, 16, lambda k: arrived(upd_ref.at[0], o2_s.at[k]))


def place(upd_hbm, mir_hbm, upd_out, mir_out, upd, mir, sem):
    reads = [
        pltpu.make_async_copy(upd_hbm, upd, sem.at[0]),
        pltpu.make_async_copy(mir_hbm, mir, sem.at[1]),
    ]
    writes = [
        pltpu.make_async_copy(upd, upd_out, sem.at[0]),
        pltpu.make_async_copy(mir, mir_out, sem.at[1]),
    ]
    for read in reads:
        read.start()
    for read, write in zip(reads, writes):
        read.wait()
        write.start()
    for write in writes:
        write.wait()


def per_device(pair, gain, wq, wk, wv, wg, bw, wo):
    bf16, f32 = jnp.bfloat16, jnp.float32
    hbm = pl.BlockSpec(memory_space=pl.ANY)
    dma = pltpu.SemaphoreType.DMA
    tile = jax.ShapeDtypeStruct(pair.shape, bf16)
    update, mirrored = pl.pallas_call(
        kernel,
        out_shape=(tile, tile),
        in_specs=[hbm] * 8,
        out_specs=(hbm, hbm),
        scratch_shapes=[
            pltpu.VMEM((16, 32, 128), bf16),
            pltpu.VMEM((1, 128), bf16),
            pltpu.VMEM((128, 128), bf16),
            pltpu.VMEM((128, 128), bf16),
            pltpu.VMEM((128, 128), bf16),
            pltpu.VMEM((128, 128), bf16),
            pltpu.VMEM((4, 128), bf16),
            pltpu.VMEM((128, 128), bf16),
            dma((8,)),
            pltpu.VMEM((16, 32, 128), bf16),
            pltpu.VMEM((128, 2048), bf16),
            pltpu.VMEM((64, 2048), bf16),
            pltpu.VMEM((8, 16, 128), bf16),
            pltpu.VMEM((2, 8, 64, 256), bf16),
            pltpu.VMEM((2, 4, 128, 256), f32),
            pltpu.VMEM((4, 512, 128), bf16),
            pltpu.VMEM((128, 128), bf16),
            pltpu.VMEM((4, 2048, 128), bf16),
            pltpu.VMEM((4, 512, 512), f32),
            pltpu.VMEM((4, 128, 2048), bf16),
            pltpu.VMEM((4, 128, 128), f32),
            pltpu.VMEM((4, 128, 128), f32),
            pltpu.VMEM((128, 128), bf16),
            pltpu.VMEM((4, 128, 128), bf16),
            pltpu.VMEM((4, 128, 128), bf16),
            pltpu.VMEM((32, 16, 128), bf16),
            pltpu.VMEM((512, 128), f32),
            pltpu.VMEM((16, 32, 128), bf16),
            dma((16,)),
            dma((16,)),
            dma((4,)),
            dma((4,)),
            dma((8,)),
            dma((8,)),
            dma((8,)),
            dma((8,)),
            dma((8,)),
            dma((8,)),
            dma((4,)),
            dma((4,)),
            dma((16,)),
            dma((16,)),
            dma((32,)),
            dma((32,)),
        ],
        compiler_params=pltpu.CompilerParams(
            collective_id=0, has_side_effects=True, vmem_limit_bytes=56 * 2**20
        ),
        cost_estimate=pl.CostEstimate(
            flops=1_000_000_000, bytes_accessed=1_000_000, transcendentals=1_100_000
        ),
    )(pair, gain.reshape(1, 128), wq, wk, wv, wg, bw.T, wo)
    return pl.pallas_call(
        place,
        out_shape=(tile, tile),
        in_specs=[hbm, hbm],
        out_specs=(hbm, hbm),
        scratch_shapes=[
            pltpu.VMEM((16, 32, 128), bf16),
            pltpu.VMEM((16, 32, 128), bf16),
            dma((2,)),
        ],
        compiler_params=pltpu.CompilerParams(vmem_limit_bytes=56 * 2**20),
        cost_estimate=pl.CostEstimate(flops=0, bytes_accessed=524288, transcendentals=0),
    )(update, mirrored)


def solution(mesh):
    placed = (P("row", "col", None), P(), P(), P(), P(), P(), P(), P())
    return jax.shard_map(
        per_device,
        mesh=mesh,
        in_specs=placed,
        out_specs=(P("row", "col", None), P("row", "col", None)),
        check_vma=False,
    )
```

```python
import jax
import jax.numpy as jnp
from jax import lax
from jax.experimental import pallas as pl
from jax.experimental.pallas import tpu as pltpu
from jax.sharding import PartitionSpec as P

EPSILON = 1e-05
MESH = pl.DeviceIdType.MESH
EARLY = 6
NT = (((1,), (1,)), ((), ()))


def dot(a, b):
    return jnp.dot(a, b, preferred_element_type=jnp.float32)


def div(a, b):
    return lax.div(a, jnp.int32(b))


def rem(a, b):
    return lax.rem(a, jnp.int32(b))


def outward(n, middle):
    return middle + div(n + 1, 2) * (1 - 2 * rem(n, 2))


def dot_nt(a, b):
    return lax.dot_general(a, b, NT, preferred_element_type=jnp.float32)


def kernel(
    pair_hbm,
    gain_hbm,
    wq_hbm,
    wk_hbm,
    wv_hbm,
    wg_hbm,
    bw_hbm,
    wo_hbm,
    upd_ref,
    mir_ref,
    pair_ref,
    gain_ref,
    wq_ref,
    wk_ref,
    wv_ref,
    wg_ref,
    bw_ref,
    wo_ref,
    in_sem,
    nrm,
    xcat,
    wbd,
    b1buf,
    bbuf,
    biasf,
    xall,
    wkt,
    vbuf,
    scores,
    weights,
    inverse,
    gbuf,
    xq,
    ustage,
    ufull,
    mstage,
    mflat,
    s1_s,
    s1_r,
    s2_s,
    s2_r,
    b1_s,
    b1_r,
    b2_s,
    b2_r,
    b3_s,
    b3_r,
    o1_s,
    o1_r,
    o2_s,
    o2_r,
    m_s,
    m_r,
):
    r = lax.axis_index("row")
    c = lax.axis_index("col")
    x = div(r, 8)
    zh = rem(div(r, 2), 4)
    core = rem(r, 2)
    y = div(c, 2)
    zl = rem(c, 2)
    z = zh * 2 + zl
    sibling = (r + 1 - 2 * core, c)

    def col_peer(k):
        return (r, rem(c + k, 16))

    def x_row(xx):
        return xx * 8 + zh * 2 + core

    def y_peer(k):
        return (r, rem(y + k, 8) * 2 + zl)

    def z_peer(k):
        zz = rem(z + k, 8)
        return (x * 8 + div(zz, 2) * 2 + core, y * 2 + rem(zz, 2))

    def send(src, dst, s_sem, r_sem, dev):
        pltpu.make_async_remote_copy(
            src_ref=src,
            dst_ref=dst,
            send_sem=s_sem,
            recv_sem=r_sem,
            device_id=dev,
            device_id_type=MESH,
        ).start()

    def arrived(ref, sem):
        pltpu.make_async_copy(ref, ref, sem).wait()

    def loop(low, high, body):
        def step(k, carry):
            body(k)
            return carry

        lax.fori_loop(low, high, step, 0)

    loads = [
        pltpu.make_async_copy(src, dst, in_sem.at[i])
        for i, (src, dst) in enumerate(
            (
                (pair_hbm, pair_ref),
                (gain_hbm, gain_ref),
                (bw_hbm, bw_ref),
                (wk_hbm, wk_ref),
                (wv_hbm, wv_ref),
                (wq_hbm, wq_ref),
                (wg_hbm, wg_ref),
                (wo_hbm, wo_ref),
            )
        )
    ]
    for load in loads[:3]:
        load.start()

    barrier = pltpu.get_barrier_semaphore()

    def greet(dev):
        pl.semaphore_signal(barrier, inc=1, device_id=dev, device_id_type=MESH)

    loop(0, 15, lambda n: greet(col_peer(outward(n, 8))))
    loop(0, 7, lambda n: greet(z_peer(outward(n, 4))))
    loop(1, 4, lambda k: greet((x_row(rem(x + k, 4)), c)))
    greet(sibling)
    for load in loads[3:]:
        load.start()

    xcat[32:128] = jnp.zeros((96, 2048), jnp.bfloat16)
    heads = lax.broadcasted_iota(jnp.int32, (64, 4), 0) // 16
    pick = heads == lax.broadcasted_iota(jnp.int32, (64, 4), 1)
    row_j = lax.broadcasted_iota(jnp.int32, (64, 128), 0) % 16
    loads[2].wait()
    spread_w = dot(pick.astype(jnp.float32).astype(jnp.bfloat16), bw_ref[...])
    for j in range(16):
        wbd[:, j * 128 : (j + 1) * 128] = jnp.where(row_j == j, spread_w, 0.0).astype(
            jnp.bfloat16
        )

    loads[1].wait()
    loads[0].wait()
    entries = pair_ref[...].reshape(512, 128).astype(jnp.float32)
    center = jnp.mean(entries, axis=-1, keepdims=True)
    shifted = entries - center
    spread = jnp.mean(shifted * shifted, axis=-1, keepdims=True)
    gain = gain_ref[...].astype(jnp.float32)
    normed = (shifted * lax.rsqrt(spread + EPSILON) * gain).astype(jnp.bfloat16)
    nrm[...] = normed.reshape(16, 32, 128)

    for j in range(16):
        xcat[0:32, j * 128 : (j + 1) * 128] = nrm[j]
    by_head = dot_nt(wbd[...], xcat[...])
    packed = by_head[0:16]
    for h in range(1, 4):
        packed = packed + pltpu.roll(by_head[16 * h : 16 * h + 16], 32 * h, 1)
    b1buf[y] = packed.astype(jnp.bfloat16)

    pl.semaphore_wait(barrier, 26)

    def send_tile(n):
        k = outward(n, 4)
        send(b1buf.at[y], b1buf.at[y], b1_s, b1_r, y_peer(k))

    loop(0, 7, send_tile)
    own_slot = pl.multiple_of((zl * 8 + y) * 32, 32)

    def send_row(n):
        k = outward(n, 8)
        send(
            nrm.at[rem(c + k, 16)],
            xall.at[0, pl.ds(own_slot, 32)],
            s1_s,
            s1_r.at[k],
            col_peer(k),
        )

    loop(0, 15, send_row)
    xall[0, pl.ds(own_slot, 32)] = nrm[c]

    def share(col):
        rows = pl.ds(pl.multiple_of((rem(col, 2) * 8 + div(col, 2)) * 32, 32), 32)
        piece = xall.at[0, rows]
        for d in (2, 1, 3):
            dev = (x_row(rem(x + d, 4)), c)
            send(piece, xall.at[d, rows], s2_s.at[d], s2_r.at[d], dev)

    def pass_row(n):
        k = outward(14 - n, 8)
        arrived(xall.at[0, pl.ds(0, 32)], s1_r.at[k])
        share(rem(c - k + 16, 16))

    share(c)
    loop(0, EARLY, pass_row)

    arrived(b1buf.at[pl.ds(0, 7)], b1_r)
    lane_group = lax.broadcasted_iota(jnp.int32, (16, 128), 1) // 32
    for g in range(2):
        tiles = [b1buf[4 * g + i].astype(jnp.float32) for i in range(4)]
        for h in range(4):
            merged = jnp.zeros((16, 128), jnp.float32)
            for i in range(4):
                turn = (i - h) * 32 % 128
                moved = pltpu.roll(tiles[i], turn, 1) if turn else tiles[i]
                merged = jnp.where(lane_group == i, moved, merged)
            bbuf[core, z, h * 16 : (h + 1) * 16, g * 128 : (g + 1) * 128] = merged.astype(
                jnp.bfloat16
            )
    own_bias = bbuf.at[core, z]

    def send_bias(n):
        k = outward(n, 4)
        send(own_bias, own_bias, b2_s.at[k], b2_r.at[k], z_peer(k))

    loop(0, 7, send_bias)
    send(own_bias, own_bias, b3_s.at[0], b3_r.at[0], sibling)

    loop(EARLY, 15, pass_row)
    loads[3].wait()
    wkt[...] = wk_ref[...].astype(jnp.float32).T.astype(jnp.bfloat16)

    def project(d):
        keys = xall[d]
        kt = dot_nt(wkt[...], keys).astype(jnp.bfloat16)
        values = dot(keys, wv_ref[...])
        for h in range(4):
            vbuf[d, h * 512 : (h + 1) * 512] = jnp.where(
                head_of_key == h, values, 0.0
            ).astype(jnp.bfloat16)
        for q in range(4):
            slot = pl.multiple_of(((q % 2) * 8 + 2 * x + q // 2) * 32, 32)
            xq[q * 32 : (q + 1) * 32] = xall[d, pl.ds(slot, 32)]
        own = xq[...]
        gbuf[d] = jax.nn.sigmoid(dot(own, wg_ref[...]))
        queries = (dot(own, wq_ref[...]) * 32**-0.5).astype(jnp.bfloat16)
        queries = queries.astype(jnp.float32)
        by_head = [
            jnp.where(head_of_lane == h, queries, 0.0).astype(jnp.bfloat16)
            for h in range(4)
        ]
        scores[d] = dot(jnp.concatenate(by_head, 0), kt)

    def lay_bias(half, zz):
        block = bbuf[half, zz].astype(jnp.float32)
        j0 = pl.multiple_of((div(zz, 2) * 2 + half) * 16, 16)
        for h in range(4):
            biasf[rem(zz, 2), h, pl.ds(j0, 16)] = block[h * 16 : (h + 1) * 16]

    head_of_lane = lax.broadcasted_iota(jnp.int32, (128, 128), 1) // 32
    head_of_key = lax.broadcasted_iota(jnp.int32, (512, 128), 1) // 32

    for load in loads[4:]:
        load.wait()
    project(0)
    lay_bias(core, z)

    def forward(n):
        k = outward(6 - n, 4)
        zz = rem(z - k + 8, 8)
        block = bbuf.at[core, zz]
        arrived(block, b2_r.at[k])
        send(block, block, b3_s.at[k], b3_r.at[k], sibling)
        lay_bias(core, zz)

    loop(0, 7, forward)

    def next_row(d):
        arrived(xall.at[d], s2_r.at[d])
        project(d)

    next_row(1)
    next_row(3)
    next_row(2)

    def take_bias(n):
        k = outward(7 - n, 4)
        zz = rem(z - k + 8, 8)
        arrived(bbuf.at[0, 0], b3_r.at[k])
        lay_bias(1 - core, zz)

    loop(0, 8, take_bias)

    def weigh(d):
        scale = jnp.zeros((128, 128), jnp.float32)
        for h in range(4):
            bias = jnp.concatenate([biasf[0, h], biasf[1, h]], 1)
            logits = scores[d, h * 128 : (h + 1) * 128] + bias
            exponent = jnp.exp(logits - jnp.max(logits, axis=-1, keepdims=True))
            denominator = jnp.sum(exponent, axis=-1, keepdims=True)
            weights[d, :, h * 512 : (h + 1) * 512] = exponent.astype(jnp.bfloat16)
            scale = jnp.where(head_of_lane == h, 1.0 / denominator, scale)
        inverse[d] = scale

    def mix(d):
        attended = dot(weights[d], vbuf[d]) * inverse[d]
        gated = (gbuf[d] * attended).astype(jnp.bfloat16)
        ustage[d] = dot(gated, wo_ref[...]).astype(jnp.bfloat16)

    def mirror_copy(d, t):
        x_i = rem(x - d + 4, 4)
        to_row = x * 8 + t
        to_col = x_i * 4 + zh
        src = ustage.at[d, pl.ds(pl.multiple_of(t * 16, 16), 16)]
        dst = mstage.at[core * 16 + c]
        here = jnp.logical_and(to_row == r, to_col == c)
        return src, dst, (to_row, to_col), here

    def emit(d):
        if d > 0:
            dev = (x_row(rem(x - d + 4, 4)), c)
            send(ustage.at[d], ufull.at[x], o1_s.at[d], o1_r.at[d], dev)

        def one(n):
            t = rem(zh * 2 + 4 + n, 8)
            src, dst, dev, here = mirror_copy(d, t)

            @pl.when(here)
            def _():
                pltpu.make_async_copy(src, dst, m_r).start()

            @pl.when(jnp.logical_not(here))
            def _():
                send(src, dst, m_s, m_r, dev)

        loop(0, 8, one)

    weigh(2)
    weigh(1)
    mix(2)
    emit(2)
    weigh(3)
    mix(1)
    emit(1)
    weigh(0)
    mix(3)
    emit(3)
    mix(0)
    emit(0)
    ufull[x] = ustage[0]

    def give(group):
        def one(q):
            cc = group * 4 + q
            src = ufull.at[group, pl.ds(pl.multiple_of(q * 32, 32), 32)]
            dst = upd_ref.at[c]

            @pl.when(cc == c)
            def _():
                pltpu.make_async_copy(src, dst, o2_r).start()

            @pl.when(cc != c)
            def _():
                send(src, dst, o2_s, o2_r, (r, cc))

        loop(0, 4, one)

    give(x)

    def pass_on(d):
        arrived(ufull.at[0], o1_r.at[d])
        give(rem(x + d, 4))

    pass_on(2)
    pass_on(1)
    pass_on(3)

    arrived(b1buf.at[pl.ds(0, 7)], b1_s)
    arrived(nrm.at[pl.ds(0, 15)], s1_s)
    loop(1, 8, lambda k: arrived(bbuf.at[0, 0], b2_s.at[k]))
    loop(0, 8, lambda k: arrived(bbuf.at[0, 0], b3_s.at[k]))
    loop(1, 4, lambda d: arrived(xall.at[0], s2_s.at[d]))
    loop(1, 4, lambda d: arrived(ustage.at[0], o1_s.at[d]))

    arrived(mstage, m_r)
    mflat[...] = mstage[...].astype(jnp.float32).reshape(512, 128)
    for j in range(16):
        mir_ref[j] = mflat[pl.ds(j, 32, stride=16), :].astype(jnp.bfloat16)

    stays = rem(c, 4) == zh

    @pl.when(stays)
    def _():
        arrived(mstage.at[pl.ds(0, 31)], m_s)

    @pl.when(jnp.logical_not(stays))
    def _():
        arrived(mstage, m_s)

    arrived(upd_ref.at[pl.ds(0, 15)], o2_s)
    arrived(upd_ref, o2_r)


def place(upd, mir, upd_out, mir_out, sem):
    writes = [
        pltpu.make_async_copy(upd, upd_out, sem.at[0]),
        pltpu.make_async_copy(mir, mir_out, sem.at[1]),
    ]
    for write in writes:
        write.start()
    for write in writes:
        write.wait()


def per_device(pair, gain, wq, wk, wv, wg, bw, wo):
    bf16, f32 = jnp.bfloat16, jnp.float32
    hbm = pl.BlockSpec(memory_space=pl.ANY)
    vmem = pl.BlockSpec(memory_space=pltpu.VMEM)
    near = pltpu.VMEM(pair.shape, bf16)
    dma = pltpu.SemaphoreType.DMA
    tile = jax.ShapeDtypeStruct(pair.shape, bf16)
    far = [
        pltpu.with_memory_space_constraint(array, pltpu.HBM)
        for array in (pair, gain.reshape(1, 128), wq, wk, wv, wg, bw.T, wo)
    ]
    update, mirrored = pl.pallas_call(
        kernel,
        out_shape=(near, near),
        in_specs=[hbm] * 8,
        out_specs=(vmem, vmem),
        scratch_shapes=[
            pltpu.VMEM((16, 32, 128), bf16),
            pltpu.VMEM((1, 128), bf16),
            pltpu.VMEM((128, 128), bf16),
            pltpu.VMEM((128, 128), bf16),
            pltpu.VMEM((128, 128), bf16),
            pltpu.VMEM((128, 128), bf16),
            pltpu.VMEM((4, 128), bf16),
            pltpu.VMEM((128, 128), bf16),
            dma((8,)),
            pltpu.VMEM((16, 32, 128), bf16),
            pltpu.VMEM((128, 2048), bf16),
            pltpu.VMEM((64, 2048), bf16),
            pltpu.VMEM((8, 16, 128), bf16),
            pltpu.VMEM((2, 8, 64, 256), bf16),
            pltpu.VMEM((2, 4, 128, 256), f32),
            pltpu.VMEM((4, 512, 128), bf16),
            pltpu.VMEM((128, 128), bf16),
            pltpu.VMEM((4, 2048, 128), bf16),
            pltpu.VMEM((4, 512, 512), f32),
            pltpu.VMEM((4, 128, 2048), bf16),
            pltpu.VMEM((4, 128, 128), f32),
            pltpu.VMEM((4, 128, 128), f32),
            pltpu.VMEM((128, 128), bf16),
            pltpu.VMEM((4, 128, 128), bf16),
            pltpu.VMEM((4, 128, 128), bf16),
            pltpu.VMEM((32, 16, 128), bf16),
            pltpu.VMEM((512, 128), f32),
            dma,
            dma((16,)),
            dma((4,)),
            dma((4,)),
            dma,
            dma,
            dma((8,)),
            dma((8,)),
            dma((8,)),
            dma((8,)),
            dma((4,)),
            dma((4,)),
            dma,
            dma,
            dma,
            dma,
        ],
        compiler_params=pltpu.CompilerParams(
            collective_id=0, has_side_effects=True, vmem_limit_bytes=32 * 2**20
        ),
        cost_estimate=pl.CostEstimate(
            flops=1_000_000_000, bytes_accessed=1_000_000, transcendentals=1_100_000
        ),
    )(*far)
    return pl.pallas_call(
        place,
        out_shape=(tile, tile),
        in_specs=[vmem, vmem],
        out_specs=(hbm, hbm),
        scratch_shapes=[dma((2,))],
        compiler_params=pltpu.CompilerParams(vmem_limit_bytes=4 * 2**20),
        cost_estimate=pl.CostEstimate(flops=0, bytes_accessed=524288, transcendentals=0),
    )(update, mirrored)


def solution(mesh):
    placed = (P("row", "col", None), P(), P(), P(), P(), P(), P(), P())
    return jax.shard_map(
        per_device,
        mesh=mesh,
        in_specs=placed,
        out_specs=(P("row", "col", None), P("row", "col", None)),
        check_vma=False,
    )
```

```python
import jax
import jax.numpy as jnp
from jax import lax
from jax.experimental import pallas as pl
from jax.experimental.pallas import tpu as pltpu
from jax.sharding import PartitionSpec as P

EPSILON = 1e-05
MESH = pl.DeviceIdType.MESH
EARLY = 6
NT = (((1,), (1,)), ((), ()))


def dot(a, b):
    return jnp.dot(a, b, preferred_element_type=jnp.float32)


def div(a, b):
    return lax.div(a, jnp.int32(b))


def rem(a, b):
    return lax.rem(a, jnp.int32(b))


def outward(n, middle):
    return middle + div(n + 1, 2) * (1 - 2 * rem(n, 2))


def position(k):
    below = 1 - div(k, 4)
    return (1 - 2 * below) * 2 * (k - 4) - below


def dot_nt(a, b):
    return lax.dot_general(a, b, NT, preferred_element_type=jnp.float32)


def kernel(
    pair_hbm,
    gain_hbm,
    wq_hbm,
    wk_hbm,
    wv_hbm,
    wg_hbm,
    bw_hbm,
    wo_hbm,
    upd_ref,
    mir_ref,
    pair_ref,
    gain_ref,
    wq_ref,
    wk_ref,
    wv_ref,
    wg_ref,
    bw_ref,
    wo_ref,
    in_sem,
    nrm,
    xcat,
    wbd,
    b1buf,
    bbuf,
    biasf,
    xall,
    wkt,
    vbuf,
    scores,
    weights,
    inverse,
    gbuf,
    xq,
    ustage,
    ufull,
    mstage,
    mflat,
    s1_s,
    s1_r,
    s2_s,
    s2_r,
    b1_s,
    b1_r,
    b2_s,
    b2_r,
    b3_s,
    b3_r,
    o1_s,
    o1_r,
    o2_s,
    o2_r,
    m_s,
    m_r,
):
    r = lax.axis_index("row")
    c = lax.axis_index("col")
    x = div(r, 8)
    zh = rem(div(r, 2), 4)
    core = rem(r, 2)
    y = div(c, 2)
    zl = rem(c, 2)
    z = zh * 2 + zl
    sibling = (r + 1 - 2 * core, c)

    def col_peer(k):
        return (r, rem(c + k, 16))

    def x_row(xx):
        return xx * 8 + zh * 2 + core

    def y_peer(k):
        return (r, rem(y + k, 8) * 2 + zl)

    def z_peer(k):
        zz = rem(z + k, 8)
        return (x * 8 + div(zz, 2) * 2 + core, y * 2 + rem(zz, 2))

    def send(src, dst, s_sem, r_sem, dev):
        pltpu.make_async_remote_copy(
            src_ref=src,
            dst_ref=dst,
            send_sem=s_sem,
            recv_sem=r_sem,
            device_id=dev,
            device_id_type=MESH,
        ).start()

    def arrived(ref, sem):
        pltpu.make_async_copy(ref, ref, sem).wait()

    def loop(low, high, body):
        def step(k, carry):
            body(k)
            return carry

        lax.fori_loop(low, high, step, 0)

    loads = [
        pltpu.make_async_copy(src, dst, in_sem.at[i])
        for i, (src, dst) in enumerate(
            (
                (pair_hbm, pair_ref),
                (gain_hbm, gain_ref),
                (bw_hbm, bw_ref),
                (wk_hbm, wk_ref),
                (wv_hbm, wv_ref),
                (wq_hbm, wq_ref),
                (wg_hbm, wg_ref),
                (wo_hbm, wo_ref),
            )
        )
    ]
    for load in loads[:3]:
        load.start()

    barrier = pltpu.get_barrier_semaphore()

    def greet(dev):
        pl.semaphore_signal(barrier, inc=1, device_id=dev, device_id_type=MESH)

    loop(0, 15, lambda n: greet(col_peer(outward(n, 8))))
    loop(0, 7, lambda n: greet(z_peer(outward(n, 4))))
    loop(1, 4, lambda k: greet((x_row(rem(x + k, 4)), c)))
    greet(sibling)
    for load in loads[3:]:
        load.start()

    xcat[32:128] = jnp.zeros((96, 2048), jnp.bfloat16)
    heads = lax.broadcasted_iota(jnp.int32, (64, 4), 0) // 16
    pick = heads == lax.broadcasted_iota(jnp.int32, (64, 4), 1)
    row_j = lax.broadcasted_iota(jnp.int32, (64, 128), 0) % 16
    loads[2].wait()
    spread_w = dot(pick.astype(jnp.float32).astype(jnp.bfloat16), bw_ref[...])
    for j in range(16):
        wbd[:, j * 128 : (j + 1) * 128] = jnp.where(row_j == j, spread_w, 0.0).astype(
            jnp.bfloat16
        )

    loads[1].wait()
    loads[0].wait()
    entries = pair_ref[...].reshape(512, 128).astype(jnp.float32)
    center = jnp.mean(entries, axis=-1, keepdims=True)
    shifted = entries - center
    spread = jnp.mean(shifted * shifted, axis=-1, keepdims=True)
    gain = gain_ref[...].astype(jnp.float32)
    normed = (shifted * lax.rsqrt(spread + EPSILON) * gain).astype(jnp.bfloat16)
    nrm[...] = normed.reshape(16, 32, 128)

    for j in range(16):
        xcat[0:32, j * 128 : (j + 1) * 128] = nrm[j]
    by_head = dot_nt(wbd[...], xcat[...])
    packed = by_head[0:16]
    for h in range(1, 4):
        packed = packed + pltpu.roll(by_head[16 * h : 16 * h + 16], 32 * h, 1)
    b1buf[7] = packed.astype(jnp.bfloat16)

    pl.semaphore_wait(barrier, 26)

    def send_tile(n):
        k = outward(n, 4)
        send(b1buf.at[7], b1buf.at[n], b1_s, b1_r.at[n], y_peer(k))

    loop(0, 7, send_tile)
    def slot_rows(z_low, k):
        return pl.ds(pl.multiple_of((z_low * 8 + position(k)) * 32, 32), 32)

    def send_row(n):
        k = outward(n, 8)
        col = rem(c + k, 16)
        send(
            nrm.at[col],
            xall.at[0, slot_rows(zl, rem(div(col, 2) - y + 8, 8))],
            s1_s,
            s1_r.at[k],
            (r, col),
        )

    loop(0, 15, send_row)
    xall[0, slot_rows(zl, jnp.int32(0))] = nrm[c]

    def share(col):
        rows = slot_rows(rem(col, 2), rem(y - div(col, 2) + 8, 8))
        piece = xall.at[0, rows]
        for d in (2, 1, 3):
            dev = (x_row(rem(x + d, 4)), c)
            send(piece, xall.at[d, rows], s2_s.at[d], s2_r.at[d], dev)

    def pass_row(n):
        k = outward(14 - n, 8)
        arrived(xall.at[0, pl.ds(0, 32)], s1_r.at[k])
        share(rem(c - k + 16, 16))

    share(c)
    lane_group = lax.broadcasted_iota(jnp.int32, (16, 128), 1) // 32

    def spread_bias(half, first, count):
        loop(first, first + count, lambda n: arrived(b1buf.at[0], b1_r.at[n]))
        tiles = [b1buf[4 * half + i].astype(jnp.float32) for i in range(4)]
        for h in range(4):
            merged = jnp.zeros((16, 128), jnp.float32)
            for i in range(4):
                turn = (i - h) * 32 % 128
                moved = pltpu.roll(tiles[i], turn, 1) if turn else tiles[i]
                merged = jnp.where(lane_group == i, moved, merged)
            bbuf[core, z, half, h * 16 : (h + 1) * 16] = merged.astype(jnp.bfloat16)
        block = bbuf.at[core, z, half]

        def send_bias(n):
            k = outward(n, 4)
            send(block, block, b2_s, b2_r.at[half * 8 + k], z_peer(k))

        loop(0, 7, send_bias)
        send(block, block, b3_s, b3_r.at[half * 8], sibling)

    spread_bias(1, 4, 3)
    loop(0, EARLY, pass_row)
    spread_bias(0, 0, 4)
    loop(EARLY, 15, pass_row)
    loads[3].wait()
    wkt[...] = wk_ref[...].astype(jnp.float32).T.astype(jnp.bfloat16)

    def project(d):
        keys = xall[d]
        kt = dot_nt(wkt[...], keys).astype(jnp.bfloat16)
        values = dot(keys, wv_ref[...])
        for h in range(4):
            vbuf[d, h * 512 : (h + 1) * 512] = jnp.where(
                head_of_key == h, values, 0.0
            ).astype(jnp.bfloat16)
        for q in range(4):
            k = rem(y - 2 * x - q // 2 + 8, 8)
            xq[q * 32 : (q + 1) * 32] = xall[d, slot_rows(q % 2, k)]
        own = xq[...]
        gbuf[d] = jax.nn.sigmoid(dot(own, wg_ref[...]))
        queries = (dot(own, wq_ref[...]) * 32**-0.5).astype(jnp.bfloat16)
        queries = queries.astype(jnp.float32)
        by_head = [
            jnp.where(head_of_lane == h, queries, 0.0).astype(jnp.bfloat16)
            for h in range(4)
        ]
        scores[d] = dot(jnp.concatenate(by_head, 0), kt)

    def lay_bias(side, zz, half):
        block = bbuf[side, zz, half].astype(jnp.float32)
        j0 = pl.multiple_of((div(zz, 2) * 2 + side) * 16, 16)
        lanes = slice(half * 128, half * 128 + 128)
        for h in range(4):
            biasf[rem(zz, 2), h, pl.ds(j0, 16), lanes] = block[h * 16 : (h + 1) * 16]

    head_of_lane = lax.broadcasted_iota(jnp.int32, (128, 128), 1) // 32
    head_of_key = lax.broadcasted_iota(jnp.int32, (512, 128), 1) // 32

    for load in loads[4:]:
        load.wait()
    project(0)
    lay_bias(core, z, 0)
    lay_bias(core, z, 1)

    def forward(half):
        def one(n):
            k = outward(6 - n, 4)
            zz = rem(z - k + 8, 8)
            block = bbuf.at[core, zz, half]
            arrived(block, b2_r.at[half * 8 + k])
            send(block, block, b3_s, b3_r.at[half * 8 + k], sibling)
            lay_bias(core, zz, half)

        loop(0, 7, one)

    def next_row(d):
        arrived(xall.at[d], s2_r.at[d])
        project(d)

    def take_bias(half):
        def one(n):
            k = outward(7 - n, 4)
            zz = rem(z - k + 8, 8)
            arrived(bbuf.at[0, 0, 0], b3_r.at[half * 8 + k])
            lay_bias(1 - core, zz, half)

        loop(0, 8, one)

    forward(1)
    next_row(1)
    next_row(3)
    forward(0)
    next_row(2)
    take_bias(1)
    take_bias(0)

    def weigh(d):
        scale = jnp.zeros((128, 128), jnp.float32)
        for h in range(4):
            bias = jnp.concatenate([biasf[0, h], biasf[1, h]], 1)
            logits = scores[d, h * 128 : (h + 1) * 128] + bias
            exponent = jnp.exp(logits - jnp.max(logits, axis=-1, keepdims=True))
            denominator = jnp.sum(exponent, axis=-1, keepdims=True)
            weights[d, :, h * 512 : (h + 1) * 512] = exponent.astype(jnp.bfloat16)
            scale = jnp.where(head_of_lane == h, 1.0 / denominator, scale)
        inverse[d] = scale

    def mix(d):
        attended = dot(weights[d], vbuf[d]) * inverse[d]
        gated = (gbuf[d] * attended).astype(jnp.bfloat16)
        ustage[d] = dot(gated, wo_ref[...]).astype(jnp.bfloat16)

    def mirror_copy(d, t):
        x_i = rem(x - d + 4, 4)
        to_row = x * 8 + t
        to_col = x_i * 4 + zh
        src = ustage.at[d, pl.ds(pl.multiple_of(t * 16, 16), 16)]
        dst = mstage.at[core * 16 + c]
        here = jnp.logical_and(to_row == r, to_col == c)
        return src, dst, (to_row, to_col), here

    def mirror_row(d, t):
        src, dst, dev, here = mirror_copy(d, t)

        @pl.when(here)
        def _():
            pltpu.make_async_copy(src, dst, m_r).start()

        @pl.when(jnp.logical_not(here))
        def _():
            send(src, dst, m_s, m_r, dev)

    def give(group):
        def one(q):
            cc = group * 4 + q
            src = ufull.at[group, pl.ds(pl.multiple_of(q * 32, 32), 32)]
            dst = upd_ref.at[c]

            @pl.when(cc == c)
            def _():
                pltpu.make_async_copy(src, dst, o2_r).start()

            @pl.when(cc != c)
            def _():
                send(src, dst, o2_s, o2_r, (r, cc))

        loop(0, 4, one)

    def emit(d):
        @pl.when(d > 0)
        def _():
            dev = (x_row(rem(x - d + 4, 4)), c)
            send(ustage.at[d], ufull.at[x], o1_s.at[d], o1_r.at[d], dev)

        loop(0, 4, lambda t: mirror_row(d, t))

        @pl.when(d == 0)
        def _():
            ufull[x] = ustage[0]
            give(x)

    far = rem(div(rem(y - div(zh, 2) + 8, 8) + 4, 2), 4)
    high = div(zh, 2)
    order = [
        d + high * (rem(x - rem(far + step, 4) + 4, 4) - d)
        for d, step in ((2, 0), (1, 1), (3, 3), (0, 2))
    ]
    weigh(order[0])
    weigh(order[1])
    mix(order[0])
    emit(order[0])
    weigh(order[2])
    mix(order[1])
    emit(order[1])
    weigh(order[3])
    mix(order[2])
    emit(order[2])
    mix(order[3])
    emit(order[3])

    def pass_on(d):
        arrived(ufull.at[0], o1_r.at[d])
        give(rem(x + d, 4))

    pass_on(2)
    pass_on(1)
    pass_on(3)
    for d in order:
        loop(4, 8, lambda t: mirror_row(d, t))

    arrived(b1buf.at[pl.ds(0, 7)], b1_s)
    arrived(nrm.at[pl.ds(0, 15)], s1_s)
    arrived(bbuf.at[0, pl.ds(0, 7)], b2_s)
    arrived(bbuf.at[0], b3_s)
    loop(1, 4, lambda d: arrived(xall.at[0], s2_s.at[d]))
    loop(1, 4, lambda d: arrived(ustage.at[0], o1_s.at[d]))

    arrived(mstage, m_r)
    mflat[...] = mstage[...].astype(jnp.float32).reshape(512, 128)
    for j in range(16):
        mir_ref[j] = mflat[pl.ds(j, 32, stride=16), :].astype(jnp.bfloat16)

    stays = rem(c, 4) == zh

    @pl.when(stays)
    def _():
        arrived(mstage.at[pl.ds(0, 31)], m_s)

    @pl.when(jnp.logical_not(stays))
    def _():
        arrived(mstage, m_s)

    arrived(upd_ref.at[pl.ds(0, 15)], o2_s)
    arrived(upd_ref, o2_r)


def place(upd, mir, upd_out, mir_out, sem):
    writes = [
        pltpu.make_async_copy(upd, upd_out, sem.at[0]),
        pltpu.make_async_copy(mir, mir_out, sem.at[1]),
    ]
    for write in writes:
        write.start()
    for write in writes:
        write.wait()


def per_device(pair, gain, wq, wk, wv, wg, bw, wo):
    bf16, f32 = jnp.bfloat16, jnp.float32
    hbm = pl.BlockSpec(memory_space=pl.ANY)
    vmem = pl.BlockSpec(memory_space=pltpu.VMEM)
    near = pltpu.VMEM(pair.shape, bf16)
    dma = pltpu.SemaphoreType.DMA
    tile = jax.ShapeDtypeStruct(pair.shape, bf16)
    far = [
        pltpu.with_memory_space_constraint(array, pltpu.HBM)
        for array in (pair, gain.reshape(1, 128), wq, wk, wv, wg, bw.T, wo)
    ]
    update, mirrored = pl.pallas_call(
        kernel,
        out_shape=(near, near),
        in_specs=[hbm] * 8,
        out_specs=(vmem, vmem),
        scratch_shapes=[
            pltpu.VMEM((16, 32, 128), bf16),
            pltpu.VMEM((1, 128), bf16),
            pltpu.VMEM((128, 128), bf16),
            pltpu.VMEM((128, 128), bf16),
            pltpu.VMEM((128, 128), bf16),
            pltpu.VMEM((128, 128), bf16),
            pltpu.VMEM((4, 128), bf16),
            pltpu.VMEM((128, 128), bf16),
            dma((8,)),
            pltpu.VMEM((16, 32, 128), bf16),
            pltpu.VMEM((128, 2048), bf16),
            pltpu.VMEM((64, 2048), bf16),
            pltpu.VMEM((8, 16, 128), bf16),
            pltpu.VMEM((2, 8, 2, 64, 128), bf16),
            pltpu.VMEM((2, 4, 128, 256), f32),
            pltpu.VMEM((4, 512, 128), bf16),
            pltpu.VMEM((128, 128), bf16),
            pltpu.VMEM((4, 2048, 128), bf16),
            pltpu.VMEM((4, 512, 512), f32),
            pltpu.VMEM((4, 128, 2048), bf16),
            pltpu.VMEM((4, 128, 128), f32),
            pltpu.VMEM((4, 128, 128), f32),
            pltpu.VMEM((128, 128), bf16),
            pltpu.VMEM((4, 128, 128), bf16),
            pltpu.VMEM((4, 128, 128), bf16),
            pltpu.VMEM((32, 16, 128), bf16),
            pltpu.VMEM((512, 128), f32),
            dma,
            dma((16,)),
            dma((4,)),
            dma((4,)),
            dma,
            dma((8,)),
            dma,
            dma((16,)),
            dma,
            dma((16,)),
            dma((4,)),
            dma((4,)),
            dma,
            dma,
            dma,
            dma,
        ],
        compiler_params=pltpu.CompilerParams(
            collective_id=0, has_side_effects=True, vmem_limit_bytes=32 * 2**20
        ),
        cost_estimate=pl.CostEstimate(
            flops=1_000_000_000, bytes_accessed=1_000_000, transcendentals=1_100_000
        ),
    )(*far)
    return pl.pallas_call(
        place,
        out_shape=(tile, tile),
        in_specs=[vmem, vmem],
        out_specs=(hbm, hbm),
        scratch_shapes=[dma((2,))],
        compiler_params=pltpu.CompilerParams(vmem_limit_bytes=4 * 2**20),
        cost_estimate=pl.CostEstimate(flops=0, bytes_accessed=524288, transcendentals=0),
    )(update, mirrored)


def solution(mesh):
    placed = (P("row", "col", None), P(), P(), P(), P(), P(), P(), P())
    return jax.shard_map(
        per_device,
        mesh=mesh,
        in_specs=placed,
        out_specs=(P("row", "col", None), P("row", "col", None)),
        check_vma=False,
    )
```

```python
import jax
import jax.numpy as jnp
from jax import lax
from jax.experimental import pallas as pl
from jax.experimental.pallas import tpu as pltpu
from jax.sharding import PartitionSpec as P

EPSILON = 1e-05
MESH = pl.DeviceIdType.MESH
EARLY = 6
NT = (((1,), (1,)), ((), ()))


def dot(a, b):
    return jnp.dot(a, b, preferred_element_type=jnp.float32)


def div(a, b):
    return lax.div(a, jnp.int32(b))


def rem(a, b):
    return lax.rem(a, jnp.int32(b))


def outward(n, middle):
    return middle + div(n + 1, 2) * (1 - 2 * rem(n, 2))


def position(k):
    below = 1 - div(k, 4)
    return (1 - 2 * below) * 2 * (k - 4) - below


def dot_nt(a, b):
    return lax.dot_general(a, b, NT, preferred_element_type=jnp.float32)


def kernel(
    pair_hbm,
    gain_hbm,
    wq_hbm,
    wk_hbm,
    wv_hbm,
    wg_hbm,
    bw_hbm,
    wo_hbm,
    upd_ref,
    mir_ref,
    pair_ref,
    gain_ref,
    wq_ref,
    wk_ref,
    wv_ref,
    wg_ref,
    bw_ref,
    wo_ref,
    in_sem,
    nrm,
    xcat,
    wbd,
    b1buf,
    bbuf,
    biasf,
    xall,
    wkt,
    vbuf,
    scores,
    weights,
    inverse,
    gbuf,
    xq,
    ustage,
    ufull,
    mstage,
    mflat,
    s1_s,
    s1_r,
    s2_s,
    s2_r,
    b1_s,
    b1_r,
    b2_s,
    b2_r,
    b3_s,
    b3_r,
    o1_s,
    o1_r,
    o2_s,
    o2_r,
    m_s,
    m_r,
):
    r = lax.axis_index("row")
    c = lax.axis_index("col")
    x = div(r, 8)
    zh = rem(div(r, 2), 4)
    core = rem(r, 2)
    y = div(c, 2)
    zl = rem(c, 2)
    z = zh * 2 + zl
    sibling = (r + 1 - 2 * core, c)

    def col_peer(k):
        return (r, rem(c + k, 16))

    def x_row(xx):
        return xx * 8 + zh * 2 + core

    def y_peer(k):
        return (r, rem(y + k, 8) * 2 + zl)

    def z_peer(k):
        zz = rem(z + k, 8)
        return (x * 8 + div(zz, 2) * 2 + core, y * 2 + rem(zz, 2))

    def send(src, dst, s_sem, r_sem, dev):
        pltpu.make_async_remote_copy(
            src_ref=src,
            dst_ref=dst,
            send_sem=s_sem,
            recv_sem=r_sem,
            device_id=dev,
            device_id_type=MESH,
        ).start()

    def arrived(ref, sem):
        pltpu.make_async_copy(ref, ref, sem).wait()

    def loop(low, high, body):
        def step(k, carry):
            body(k)
            return carry

        lax.fori_loop(low, high, step, 0)

    loads = [
        pltpu.make_async_copy(src, dst, in_sem.at[i])
        for i, (src, dst) in enumerate(
            (
                (pair_hbm, pair_ref),
                (gain_hbm, gain_ref),
                (bw_hbm, bw_ref),
                (wk_hbm, wk_ref),
                (wv_hbm, wv_ref),
                (wq_hbm, wq_ref),
                (wg_hbm, wg_ref),
                (wo_hbm, wo_ref),
            )
        )
    ]
    for load in loads[:3]:
        load.start()

    barrier = pltpu.get_barrier_semaphore()

    def greet(dev):
        pl.semaphore_signal(barrier, inc=1, device_id=dev, device_id_type=MESH)

    loop(0, 15, lambda n: greet(col_peer(outward(n, 8))))
    loop(0, 7, lambda n: greet(z_peer(outward(n, 4))))
    loop(1, 4, lambda k: greet((x_row(rem(x + k, 4)), c)))
    greet(sibling)
    for load in loads[3:]:
        load.start()

    xcat[32:128] = jnp.zeros((96, 2048), jnp.bfloat16)
    heads = lax.broadcasted_iota(jnp.int32, (64, 4), 0) // 16
    pick = heads == lax.broadcasted_iota(jnp.int32, (64, 4), 1)
    row_j = lax.broadcasted_iota(jnp.int32, (64, 128), 0) % 16
    loads[2].wait()
    spread_w = dot(pick.astype(jnp.float32).astype(jnp.bfloat16), bw_ref[...])
    for j in range(16):
        wbd[:, j * 128 : (j + 1) * 128] = jnp.where(row_j == j, spread_w, 0.0).astype(
            jnp.bfloat16
        )

    loads[1].wait()
    loads[0].wait()
    entries = pair_ref[...].reshape(512, 128).astype(jnp.float32)
    center = jnp.mean(entries, axis=-1, keepdims=True)
    shifted = entries - center
    spread = jnp.mean(shifted * shifted, axis=-1, keepdims=True)
    gain = gain_ref[...].astype(jnp.float32)
    normed = (shifted * lax.rsqrt(spread + EPSILON) * gain).astype(jnp.bfloat16)
    nrm[...] = normed.reshape(16, 32, 128)

    for j in range(16):
        xcat[0:32, j * 128 : (j + 1) * 128] = nrm[j]
    by_head = dot_nt(wbd[...], xcat[...])
    packed = by_head[0:16]
    for h in range(1, 4):
        packed = packed + pltpu.roll(by_head[16 * h : 16 * h + 16], 32 * h, 1)
    b1buf[7] = packed.astype(jnp.bfloat16)

    pl.semaphore_wait(barrier, 26)

    def send_tile(n):
        k = outward(n, 4)
        send(b1buf.at[7], b1buf.at[n], b1_s, b1_r.at[n], y_peer(k))

    loop(0, 7, send_tile)
    def slot_rows(z_low, k):
        return pl.ds(pl.multiple_of((z_low * 8 + position(k)) * 32, 32), 32)

    def send_row(n):
        k = outward(n, 8)
        col = rem(c + k, 16)
        send(
            nrm.at[col],
            xall.at[0, slot_rows(zl, rem(div(col, 2) - y + 8, 8))],
            s1_s,
            s1_r.at[k],
            (r, col),
        )

    loop(0, 15, send_row)
    xall[0, slot_rows(zl, jnp.int32(0))] = nrm[c]

    def share(col):
        rows = slot_rows(rem(col, 2), rem(y - div(col, 2) + 8, 8))
        piece = xall.at[0, rows]
        for d in (2, 1, 3):
            dev = (x_row(rem(x + d, 4)), c)
            send(piece, xall.at[d, rows], s2_s.at[d], s2_r.at[d], dev)

    def pass_row(n):
        k = outward(14 - n, 8)
        arrived(xall.at[0, pl.ds(0, 32)], s1_r.at[k])
        share(rem(c - k + 16, 16))

    share(c)
    lane_group = lax.broadcasted_iota(jnp.int32, (16, 128), 1) // 32

    def spread_bias(half, first, count):
        loop(first, first + count, lambda n: arrived(b1buf.at[0], b1_r.at[n]))
        tiles = [b1buf[4 * half + i].astype(jnp.float32) for i in range(4)]
        for h in range(4):
            merged = jnp.zeros((16, 128), jnp.float32)
            for i in range(4):
                turn = (i - h) * 32 % 128
                moved = pltpu.roll(tiles[i], turn, 1) if turn else tiles[i]
                merged = jnp.where(lane_group == i, moved, merged)
            bbuf[core, z, half, h * 16 : (h + 1) * 16] = merged.astype(jnp.bfloat16)
        block = bbuf.at[core, z, half]

        def send_bias(n):
            k = outward(n, 4)
            send(block, block, b2_s, b2_r.at[half * 8 + k], z_peer(k))

        loop(0, 7, send_bias)
        send(block, block, b3_s, b3_r.at[half * 8], sibling)

    spread_bias(1, 4, 3)
    loop(0, EARLY, pass_row)
    spread_bias(0, 0, 4)
    loop(EARLY, 15, pass_row)
    loads[3].wait()
    wkt[...] = wk_ref[...].astype(jnp.float32).T.astype(jnp.bfloat16)

    def project(d):
        keys = xall[d]
        kt = dot_nt(wkt[...], keys).astype(jnp.bfloat16)
        values = dot(keys, wv_ref[...])
        for h in range(4):
            vbuf[d, h * 512 : (h + 1) * 512] = jnp.where(
                head_of_key == h, values, 0.0
            ).astype(jnp.bfloat16)
        for q in range(4):
            k = rem(y - 2 * x - q // 2 + 8, 8)
            xq[q * 32 : (q + 1) * 32] = xall[d, slot_rows(q % 2, k)]
        own = xq[...]
        gbuf[d] = jax.nn.sigmoid(dot(own, wg_ref[...]))
        queries = (dot(own, wq_ref[...]) * 32**-0.5).astype(jnp.bfloat16)
        queries = queries.astype(jnp.float32)
        by_head = [
            jnp.where(head_of_lane == h, queries, 0.0).astype(jnp.bfloat16)
            for h in range(4)
        ]
        scores[d] = dot(jnp.concatenate(by_head, 0), kt)

    def lay_bias(side, zz, half):
        block = bbuf[side, zz, half].astype(jnp.float32)
        j0 = pl.multiple_of((div(zz, 2) * 2 + side) * 16, 16)
        lanes = slice(half * 128, half * 128 + 128)
        for h in range(4):
            biasf[rem(zz, 2), h, pl.ds(j0, 16), lanes] = block[h * 16 : (h + 1) * 16]

    head_of_lane = lax.broadcasted_iota(jnp.int32, (128, 128), 1) // 32
    head_of_key = lax.broadcasted_iota(jnp.int32, (512, 128), 1) // 32

    for load in loads[4:]:
        load.wait()

    def forward(half):
        def one(n):
            k = outward(6 - n, 4)
            zz = rem(z - k + 8, 8)
            block = bbuf.at[core, zz, half]
            arrived(block, b2_r.at[half * 8 + k])
            send(block, block, b3_s, b3_r.at[half * 8 + k], sibling)

        loop(0, 7, one)
        loop(1, 8, lambda k: lay_bias(core, rem(z + k, 8), half))

    def next_row(d):
        arrived(xall.at[d], s2_r.at[d])
        project(d)

    def take_bias(half):
        def one(n):
            k = outward(7 - n, 4)
            zz = rem(z - k + 8, 8)
            arrived(bbuf.at[0, 0, 0], b3_r.at[half * 8 + k])
            lay_bias(1 - core, zz, half)

        loop(0, 8, one)

    forward(1)
    lay_bias(core, z, 0)
    lay_bias(core, z, 1)
    project(0)
    forward(0)
    next_row(1)
    next_row(3)
    next_row(2)
    take_bias(1)
    take_bias(0)

    def weigh(d):
        scale = jnp.zeros((128, 128), jnp.float32)
        for h in range(4):
            bias = jnp.concatenate([biasf[0, h], biasf[1, h]], 1)
            logits = scores[d, h * 128 : (h + 1) * 128] + bias
            exponent = jnp.exp(logits - jnp.max(logits, axis=-1, keepdims=True))
            denominator = jnp.sum(exponent, axis=-1, keepdims=True)
            weights[d, :, h * 512 : (h + 1) * 512] = exponent.astype(jnp.bfloat16)
            scale = jnp.where(head_of_lane == h, 1.0 / denominator, scale)
        inverse[d] = scale

    def mix(d):
        attended = dot(weights[d], vbuf[d]) * inverse[d]
        gated = (gbuf[d] * attended).astype(jnp.bfloat16)
        ustage[d] = dot(gated, wo_ref[...]).astype(jnp.bfloat16)

    def mirror_copy(d, t):
        x_i = rem(x - d + 4, 4)
        to_row = x * 8 + t
        to_col = x_i * 4 + zh
        src = ustage.at[d, pl.ds(pl.multiple_of(t * 16, 16), 16)]
        dst = mstage.at[core * 16 + c]
        here = jnp.logical_and(to_row == r, to_col == c)
        return src, dst, (to_row, to_col), here

    def mirror_row(d, t):
        src, dst, dev, here = mirror_copy(d, t)

        @pl.when(here)
        def _():
            pltpu.make_async_copy(src, dst, m_r).start()

        @pl.when(jnp.logical_not(here))
        def _():
            send(src, dst, m_s, m_r, dev)

    def give(group):
        def one(q):
            cc = group * 4 + q
            src = ufull.at[group, pl.ds(pl.multiple_of(q * 32, 32), 32)]
            dst = upd_ref.at[c]

            @pl.when(cc == c)
            def _():
                pltpu.make_async_copy(src, dst, o2_r).start()

            @pl.when(cc != c)
            def _():
                send(src, dst, o2_s, o2_r, (r, cc))

        loop(0, 4, one)

    def emit(d):
        @pl.when(d > 0)
        def _():
            dev = (x_row(rem(x - d + 4, 4)), c)
            send(ustage.at[d], ufull.at[x], o1_s.at[d], o1_r.at[d], dev)

        loop(0, 4, lambda t: mirror_row(d, t))

        @pl.when(d == 0)
        def _():
            ufull[x] = ustage[0]
            give(x)

    far = rem(div(rem(y - div(zh, 2) + 8, 8) + 4, 2), 4)
    high = div(zh, 2)
    order = [
        d + high * (rem(x - rem(far + step, 4) + 4, 4) - d)
        for d, step in ((2, 0), (1, 1), (3, 3), (0, 2))
    ]
    weigh(order[0])
    weigh(order[1])
    mix(order[0])
    emit(order[0])
    weigh(order[2])
    mix(order[1])
    emit(order[1])
    weigh(order[3])
    mix(order[2])
    emit(order[2])
    mix(order[3])
    emit(order[3])

    def pass_on(d):
        arrived(ufull.at[0], o1_r.at[d])
        give(rem(x + d, 4))

    pass_on(2)
    pass_on(1)
    pass_on(3)
    for d in order:
        loop(4, 8, lambda t: mirror_row(d, t))

    arrived(b1buf.at[pl.ds(0, 7)], b1_s)
    arrived(nrm.at[pl.ds(0, 15)], s1_s)
    arrived(bbuf.at[0, pl.ds(0, 7)], b2_s)
    arrived(bbuf.at[0], b3_s)
    loop(1, 4, lambda d: arrived(xall.at[0], s2_s.at[d]))
    loop(1, 4, lambda d: arrived(ustage.at[0], o1_s.at[d]))

    arrived(mstage, m_r)
    mflat[...] = mstage[...].astype(jnp.float32).reshape(512, 128)
    for j in range(16):
        mir_ref[j] = mflat[pl.ds(j, 32, stride=16), :].astype(jnp.bfloat16)

    stays = rem(c, 4) == zh

    @pl.when(stays)
    def _():
        arrived(mstage.at[pl.ds(0, 31)], m_s)

    @pl.when(jnp.logical_not(stays))
    def _():
        arrived(mstage, m_s)

    arrived(upd_ref.at[pl.ds(0, 15)], o2_s)
    arrived(upd_ref, o2_r)


def place(upd, mir, upd_out, mir_out, sem):
    writes = [
        pltpu.make_async_copy(upd, upd_out, sem.at[0]),
        pltpu.make_async_copy(mir, mir_out, sem.at[1]),
    ]
    for write in writes:
        write.start()
    for write in writes:
        write.wait()


def per_device(pair, gain, wq, wk, wv, wg, bw, wo):
    bf16, f32 = jnp.bfloat16, jnp.float32
    hbm = pl.BlockSpec(memory_space=pl.ANY)
    vmem = pl.BlockSpec(memory_space=pltpu.VMEM)
    near = pltpu.VMEM(pair.shape, bf16)
    dma = pltpu.SemaphoreType.DMA
    tile = jax.ShapeDtypeStruct(pair.shape, bf16)
    far = [
        pltpu.with_memory_space_constraint(array, pltpu.HBM)
        for array in (pair, gain.reshape(1, 128), wq, wk, wv, wg, bw.T, wo)
    ]
    update, mirrored = pl.pallas_call(
        kernel,
        out_shape=(near, near),
        in_specs=[hbm] * 8,
        out_specs=(vmem, vmem),
        scratch_shapes=[
            pltpu.VMEM((16, 32, 128), bf16),
            pltpu.VMEM((1, 128), bf16),
            pltpu.VMEM((128, 128), bf16),
            pltpu.VMEM((128, 128), bf16),
            pltpu.VMEM((128, 128), bf16),
            pltpu.VMEM((128, 128), bf16),
            pltpu.VMEM((4, 128), bf16),
            pltpu.VMEM((128, 128), bf16),
            dma((8,)),
            pltpu.VMEM((16, 32, 128), bf16),
            pltpu.VMEM((128, 2048), bf16),
            pltpu.VMEM((64, 2048), bf16),
            pltpu.VMEM((8, 16, 128), bf16),
            pltpu.VMEM((2, 8, 2, 64, 128), bf16),
            pltpu.VMEM((2, 4, 128, 256), f32),
            pltpu.VMEM((4, 512, 128), bf16),
            pltpu.VMEM((128, 128), bf16),
            pltpu.VMEM((4, 2048, 128), bf16),
            pltpu.VMEM((4, 512, 512), f32),
            pltpu.VMEM((4, 128, 2048), bf16),
            pltpu.VMEM((4, 128, 128), f32),
            pltpu.VMEM((4, 128, 128), f32),
            pltpu.VMEM((128, 128), bf16),
            pltpu.VMEM((4, 128, 128), bf16),
            pltpu.VMEM((4, 128, 128), bf16),
            pltpu.VMEM((32, 16, 128), bf16),
            pltpu.VMEM((512, 128), f32),
            dma,
            dma((16,)),
            dma((4,)),
            dma((4,)),
            dma,
            dma((8,)),
            dma,
            dma((16,)),
            dma,
            dma((16,)),
            dma((4,)),
            dma((4,)),
            dma,
            dma,
            dma,
            dma,
        ],
        compiler_params=pltpu.CompilerParams(
            collective_id=0, has_side_effects=True, vmem_limit_bytes=32 * 2**20
        ),
        cost_estimate=pl.CostEstimate(
            flops=1_000_000_000, bytes_accessed=1_000_000, transcendentals=1_100_000
        ),
    )(*far)
    return pl.pallas_call(
        place,
        out_shape=(tile, tile),
        in_specs=[vmem, vmem],
        out_specs=(hbm, hbm),
        scratch_shapes=[dma((2,))],
        compiler_params=pltpu.CompilerParams(vmem_limit_bytes=4 * 2**20),
        cost_estimate=pl.CostEstimate(flops=0, bytes_accessed=524288, transcendentals=0),
    )(update, mirrored)


def solution(mesh):
    placed = (P("row", "col", None), P(), P(), P(), P(), P(), P(), P())
    return jax.shard_map(
        per_device,
        mesh=mesh,
        in_specs=placed,
        out_specs=(P("row", "col", None), P("row", "col", None)),
        check_vma=False,
    )
```

```python
import jax
import jax.numpy as jnp
from jax import lax
from jax.experimental import pallas as pl
from jax.experimental.pallas import tpu as pltpu
from jax.sharding import PartitionSpec as P

EPSILON = 1e-05
MESH = pl.DeviceIdType.MESH
EARLY = 6
NT = (((1,), (1,)), ((), ()))


def dot(a, b):
    return jnp.dot(a, b, preferred_element_type=jnp.float32)


def div(a, b):
    return lax.div(a, jnp.int32(b))


def rem(a, b):
    return lax.rem(a, jnp.int32(b))


def outward(n, middle):
    return middle + div(n + 1, 2) * (1 - 2 * rem(n, 2))


def position(k):
    below = 1 - div(k, 4)
    return (1 - 2 * below) * 2 * (k - 4) - below


def dot_nt(a, b):
    return lax.dot_general(a, b, NT, preferred_element_type=jnp.float32)


def kernel(
    pair_hbm,
    gain_hbm,
    wq_hbm,
    wk_hbm,
    wv_hbm,
    wg_hbm,
    bw_hbm,
    wo_hbm,
    upd_ref,
    mir_ref,
    pair_ref,
    gain_ref,
    wq_ref,
    wk_ref,
    wv_ref,
    wg_ref,
    bw_ref,
    wo_ref,
    in_sem,
    nrm,
    xcat,
    wbd,
    b1buf,
    bbuf,
    biasf,
    xall,
    wkt,
    vbuf,
    scores,
    weights,
    inverse,
    gbuf,
    xq,
    ustage,
    ufull,
    mstage,
    mflat,
    s1_s,
    s1_r,
    s2_s,
    s2_r,
    b1_s,
    b1_r,
    b2_s,
    b2_r,
    b3_s,
    b3_r,
    o1_s,
    o1_r,
    o2_s,
    o2_r,
    m_s,
    m_r,
):
    r = lax.axis_index("row")
    c = lax.axis_index("col")
    x = div(r, 8)
    zh = rem(div(r, 2), 4)
    core = rem(r, 2)
    y = div(c, 2)
    zl = rem(c, 2)
    z = zh * 2 + zl
    sibling = (r + 1 - 2 * core, c)

    def col_peer(k):
        return (r, rem(c + k, 16))

    def x_row(xx):
        return xx * 8 + zh * 2 + core

    def y_peer(k):
        return (r, rem(y + k, 8) * 2 + zl)

    def z_peer(k):
        zz = rem(z + k, 8)
        return (x * 8 + div(zz, 2) * 2 + core, y * 2 + rem(zz, 2))

    def send(src, dst, s_sem, r_sem, dev):
        pltpu.make_async_remote_copy(
            src_ref=src,
            dst_ref=dst,
            send_sem=s_sem,
            recv_sem=r_sem,
            device_id=dev,
            device_id_type=MESH,
        ).start()

    def arrived(ref, sem):
        pltpu.make_async_copy(ref, ref, sem).wait()

    def loop(low, high, body):
        def step(k, carry):
            body(k)
            return carry

        lax.fori_loop(low, high, step, 0)

    loads = [
        pltpu.make_async_copy(src, dst, in_sem.at[i])
        for i, (src, dst) in enumerate(
            (
                (pair_hbm, pair_ref),
                (gain_hbm, gain_ref),
                (bw_hbm, bw_ref),
                (wk_hbm, wk_ref),
                (wv_hbm, wv_ref),
                (wq_hbm, wq_ref),
                (wg_hbm, wg_ref),
                (wo_hbm, wo_ref),
            )
        )
    ]
    for load in loads[:3]:
        load.start()

    barrier = pltpu.get_barrier_semaphore()

    def greet(dev):
        pl.semaphore_signal(barrier, inc=1, device_id=dev, device_id_type=MESH)

    loop(0, 15, lambda n: greet(col_peer(outward(n, 8))))
    loop(0, 7, lambda n: greet(z_peer(outward(n, 4))))
    loop(1, 4, lambda k: greet((x_row(rem(x + k, 4)), c)))
    greet(sibling)
    for load in loads[3:]:
        load.start()

    xcat[32:128] = jnp.zeros((96, 2048), jnp.bfloat16)
    heads = lax.broadcasted_iota(jnp.int32, (64, 4), 0) // 16
    pick = heads == lax.broadcasted_iota(jnp.int32, (64, 4), 1)
    row_j = lax.broadcasted_iota(jnp.int32, (64, 128), 0) % 16
    loads[2].wait()
    spread_w = dot(pick.astype(jnp.float32).astype(jnp.bfloat16), bw_ref[...])
    for j in range(16):
        wbd[:, j * 128 : (j + 1) * 128] = jnp.where(row_j == j, spread_w, 0.0).astype(
            jnp.bfloat16
        )

    loads[1].wait()
    loads[0].wait()
    entries = pair_ref[...].reshape(512, 128).astype(jnp.float32)
    center = jnp.mean(entries, axis=-1, keepdims=True)
    shifted = entries - center
    spread = jnp.mean(shifted * shifted, axis=-1, keepdims=True)
    gain = gain_ref[...].astype(jnp.float32)
    normed = (shifted * lax.rsqrt(spread + EPSILON) * gain).astype(jnp.bfloat16)
    nrm[...] = normed.reshape(16, 32, 128)

    for j in range(16):
        xcat[0:32, j * 128 : (j + 1) * 128] = nrm[j]
    by_head = dot_nt(wbd[...], xcat[...])
    packed = by_head[0:16]
    for h in range(1, 4):
        packed = packed + pltpu.roll(by_head[16 * h : 16 * h + 16], 32 * h, 1)
    b1buf[7] = packed.astype(jnp.bfloat16)

    pl.semaphore_wait(barrier, 26)

    def send_tile(n):
        k = outward(n, 4)
        send(b1buf.at[7], b1buf.at[n], b1_s, b1_r.at[n], y_peer(k))

    loop(0, 7, send_tile)
    def slot_rows(z_low, k):
        return pl.ds(pl.multiple_of((z_low * 8 + position(k)) * 32, 32), 32)

    def send_row(n):
        k = outward(14 - n, 8)
        col = rem(c + k, 16)
        send(
            nrm.at[col],
            xall.at[0, slot_rows(zl, rem(div(col, 2) - y + 8, 8))],
            s1_s,
            s1_r.at[k],
            (r, col),
        )

    loop(0, 15, send_row)
    xall[0, slot_rows(zl, jnp.int32(0))] = nrm[c]

    def share(col):
        rows = slot_rows(rem(col, 2), rem(y - div(col, 2) + 8, 8))
        piece = xall.at[0, rows]
        for d in (2, 1, 3):
            dev = (x_row(rem(x + d, 4)), c)
            send(piece, xall.at[d, rows], s2_s.at[d], s2_r.at[d], dev)

    def pass_row(n):
        k = outward(14 - n, 8)
        arrived(xall.at[0, pl.ds(0, 32)], s1_r.at[k])
        share(rem(c - k + 16, 16))

    share(c)
    lane_group = lax.broadcasted_iota(jnp.int32, (16, 128), 1) // 32

    def spread_bias(half, first, count):
        loop(first, first + count, lambda n: arrived(b1buf.at[0], b1_r.at[n]))
        tiles = [b1buf[4 * half + i].astype(jnp.float32) for i in range(4)]
        for h in range(4):
            merged = jnp.zeros((16, 128), jnp.float32)
            for i in range(4):
                turn = (i - h) * 32 % 128
                moved = pltpu.roll(tiles[i], turn, 1) if turn else tiles[i]
                merged = jnp.where(lane_group == i, moved, merged)
            bbuf[core, z, half, h * 16 : (h + 1) * 16] = merged.astype(jnp.bfloat16)
        block = bbuf.at[core, z, half]

        def send_bias(n):
            k = outward(n, 4)
            send(block, block, b2_s, b2_r.at[half * 8 + k], z_peer(k))

        loop(0, 7, send_bias)
        send(block, block, b3_s, b3_r.at[half * 8], sibling)

    spread_bias(1, 4, 3)
    loop(0, EARLY, pass_row)
    spread_bias(0, 0, 4)
    loop(EARLY, 15, pass_row)
    loads[3].wait()
    wkt[...] = wk_ref[...].astype(jnp.float32).T.astype(jnp.bfloat16)

    def project(d):
        keys = xall[d]
        kt = dot_nt(wkt[...], keys).astype(jnp.bfloat16)
        values = dot(keys, wv_ref[...])
        for h in range(4):
            vbuf[d, h * 512 : (h + 1) * 512] = jnp.where(
                head_of_key == h, values, 0.0
            ).astype(jnp.bfloat16)
        for q in range(4):
            k = rem(y - 2 * x - q // 2 + 8, 8)
            xq[q * 32 : (q + 1) * 32] = xall[d, slot_rows(q % 2, k)]
        own = xq[...]
        gbuf[d] = jax.nn.sigmoid(dot(own, wg_ref[...]))
        queries = (dot(own, wq_ref[...]) * 32**-0.5).astype(jnp.bfloat16)
        queries = queries.astype(jnp.float32)
        by_head = [
            jnp.where(head_of_lane == h, queries, 0.0).astype(jnp.bfloat16)
            for h in range(4)
        ]
        scores[d] = dot(jnp.concatenate(by_head, 0), kt)

    def lay_bias(side, zz, half):
        block = bbuf[side, zz, half].astype(jnp.float32)
        j0 = pl.multiple_of((div(zz, 2) * 2 + side) * 16, 16)
        lanes = slice(half * 128, half * 128 + 128)
        for h in range(4):
            biasf[rem(zz, 2), h, pl.ds(j0, 16), lanes] = block[h * 16 : (h + 1) * 16]

    head_of_lane = lax.broadcasted_iota(jnp.int32, (128, 128), 1) // 32
    head_of_key = lax.broadcasted_iota(jnp.int32, (512, 128), 1) // 32

    for load in loads[4:]:
        load.wait()

    def forward(half):
        def one(n):
            k = outward(6 - n, 4)
            zz = rem(z - k + 8, 8)
            block = bbuf.at[core, zz, half]
            arrived(block, b2_r.at[half * 8 + k])
            send(block, block, b3_s, b3_r.at[half * 8 + k], sibling)

        loop(0, 7, one)
        loop(1, 8, lambda k: lay_bias(core, rem(z + k, 8), half))

    def next_row(d):
        arrived(xall.at[d], s2_r.at[d])
        project(d)

    def take_bias(half):
        def one(n):
            k = outward(7 - n, 4)
            zz = rem(z - k + 8, 8)
            arrived(bbuf.at[0, 0, 0], b3_r.at[half * 8 + k])
            lay_bias(1 - core, zz, half)

        loop(0, 8, one)

    forward(1)
    lay_bias(core, z, 0)
    lay_bias(core, z, 1)
    project(0)
    forward(0)
    next_row(1)
    next_row(3)
    next_row(2)
    take_bias(1)
    take_bias(0)

    def weigh(d):
        scale = jnp.zeros((128, 128), jnp.float32)
        for h in range(4):
            bias = jnp.concatenate([biasf[0, h], biasf[1, h]], 1)
            logits = scores[d, h * 128 : (h + 1) * 128] + bias
            exponent = jnp.exp(logits - jnp.max(logits, axis=-1, keepdims=True))
            denominator = jnp.sum(exponent, axis=-1, keepdims=True)
            weights[d, :, h * 512 : (h + 1) * 512] = exponent.astype(jnp.bfloat16)
            scale = jnp.where(head_of_lane == h, 1.0 / denominator, scale)
        inverse[d] = scale

    def mix(d):
        attended = dot(weights[d], vbuf[d]) * inverse[d]
        gated = (gbuf[d] * attended).astype(jnp.bfloat16)
        ustage[d] = dot(gated, wo_ref[...]).astype(jnp.bfloat16)

    def mirror_copy(d, t):
        x_i = rem(x - d + 4, 4)
        to_row = x * 8 + t
        to_col = x_i * 4 + zh
        src = ustage.at[d, pl.ds(pl.multiple_of(t * 16, 16), 16)]
        dst = mstage.at[core * 16 + c]
        here = jnp.logical_and(to_row == r, to_col == c)
        return src, dst, (to_row, to_col), here

    def mirror_row(d, t):
        src, dst, dev, here = mirror_copy(d, t)

        @pl.when(here)
        def _():
            pltpu.make_async_copy(src, dst, m_r).start()

        @pl.when(jnp.logical_not(here))
        def _():
            send(src, dst, m_s, m_r, dev)

    def give(group):
        def one(q):
            cc = group * 4 + q
            src = ufull.at[group, pl.ds(pl.multiple_of(q * 32, 32), 32)]
            dst = upd_ref.at[c]

            @pl.when(cc == c)
            def _():
                pltpu.make_async_copy(src, dst, o2_r).start()

            @pl.when(cc != c)
            def _():
                send(src, dst, o2_s, o2_r, (r, cc))

        loop(0, 4, one)

    def emit(d):
        @pl.when(d > 0)
        def _():
            dev = (x_row(rem(x - d + 4, 4)), c)
            send(ustage.at[d], ufull.at[x], o1_s.at[d], o1_r.at[d], dev)

        loop(0, 4, lambda t: mirror_row(d, t))

        @pl.when(d == 0)
        def _():
            ufull[x] = ustage[0]
            give(x)

    far = rem(div(rem(y - div(zh, 2) + 8, 8) + 4, 2), 4)
    high = div(zh, 2)
    order = [
        d + high * (rem(x - rem(far + step, 4) + 4, 4) - d)
        for d, step in ((2, 0), (1, 1), (3, 3), (0, 2))
    ]
    weigh(order[0])
    mix(order[0])
    emit(order[0])
    weigh(order[1])
    weigh(order[2])
    mix(order[1])
    emit(order[1])
    weigh(order[3])
    mix(order[2])
    emit(order[2])
    mix(order[3])
    emit(order[3])

    def pass_on(d):
        arrived(ufull.at[0], o1_r.at[d])
        give(rem(x + d, 4))

    pass_on(2)
    pass_on(1)
    pass_on(3)
    for d in order:
        loop(4, 8, lambda t: mirror_row(d, t))

    arrived(b1buf.at[pl.ds(0, 7)], b1_s)
    arrived(nrm.at[pl.ds(0, 15)], s1_s)
    arrived(bbuf.at[0, pl.ds(0, 7)], b2_s)
    arrived(bbuf.at[0], b3_s)
    loop(1, 4, lambda d: arrived(xall.at[0], s2_s.at[d]))
    loop(1, 4, lambda d: arrived(ustage.at[0], o1_s.at[d]))

    arrived(mstage, m_r)
    mflat[...] = mstage[...].astype(jnp.float32).reshape(512, 128)
    for j in range(16):
        mir_ref[j] = mflat[pl.ds(j, 32, stride=16), :].astype(jnp.bfloat16)

    stays = rem(c, 4) == zh

    @pl.when(stays)
    def _():
        arrived(mstage.at[pl.ds(0, 31)], m_s)

    @pl.when(jnp.logical_not(stays))
    def _():
        arrived(mstage, m_s)

    arrived(upd_ref.at[pl.ds(0, 15)], o2_s)
    arrived(upd_ref, o2_r)


def place(upd, mir, upd_out, mir_out, sem):
    writes = [
        pltpu.make_async_copy(upd, upd_out, sem.at[0]),
        pltpu.make_async_copy(mir, mir_out, sem.at[1]),
    ]
    for write in writes:
        write.start()
    for write in writes:
        write.wait()


def per_device(pair, gain, wq, wk, wv, wg, bw, wo):
    bf16, f32 = jnp.bfloat16, jnp.float32
    hbm = pl.BlockSpec(memory_space=pl.ANY)
    vmem = pl.BlockSpec(memory_space=pltpu.VMEM)
    near = pltpu.VMEM(pair.shape, bf16)
    dma = pltpu.SemaphoreType.DMA
    tile = jax.ShapeDtypeStruct(pair.shape, bf16)
    far = [
        pltpu.with_memory_space_constraint(array, pltpu.HBM)
        for array in (pair, gain.reshape(1, 128), wq, wk, wv, wg, bw.T, wo)
    ]
    update, mirrored = pl.pallas_call(
        kernel,
        out_shape=(near, near),
        in_specs=[hbm] * 8,
        out_specs=(vmem, vmem),
        scratch_shapes=[
            pltpu.VMEM((16, 32, 128), bf16),
            pltpu.VMEM((1, 128), bf16),
            pltpu.VMEM((128, 128), bf16),
            pltpu.VMEM((128, 128), bf16),
            pltpu.VMEM((128, 128), bf16),
            pltpu.VMEM((128, 128), bf16),
            pltpu.VMEM((4, 128), bf16),
            pltpu.VMEM((128, 128), bf16),
            dma((8,)),
            pltpu.VMEM((16, 32, 128), bf16),
            pltpu.VMEM((128, 2048), bf16),
            pltpu.VMEM((64, 2048), bf16),
            pltpu.VMEM((8, 16, 128), bf16),
            pltpu.VMEM((2, 8, 2, 64, 128), bf16),
            pltpu.VMEM((2, 4, 128, 256), f32),
            pltpu.VMEM((4, 512, 128), bf16),
            pltpu.VMEM((128, 128), bf16),
            pltpu.VMEM((4, 2048, 128), bf16),
            pltpu.VMEM((4, 512, 512), f32),
            pltpu.VMEM((4, 128, 2048), bf16),
            pltpu.VMEM((4, 128, 128), f32),
            pltpu.VMEM((4, 128, 128), f32),
            pltpu.VMEM((128, 128), bf16),
            pltpu.VMEM((4, 128, 128), bf16),
            pltpu.VMEM((4, 128, 128), bf16),
            pltpu.VMEM((32, 16, 128), bf16),
            pltpu.VMEM((512, 128), f32),
            dma,
            dma((16,)),
            dma((4,)),
            dma((4,)),
            dma,
            dma((8,)),
            dma,
            dma((16,)),
            dma,
            dma((16,)),
            dma((4,)),
            dma((4,)),
            dma,
            dma,
            dma,
            dma,
        ],
        compiler_params=pltpu.CompilerParams(
            collective_id=0, has_side_effects=True, vmem_limit_bytes=32 * 2**20
        ),
        cost_estimate=pl.CostEstimate(
            flops=1_000_000_000, bytes_accessed=1_000_000, transcendentals=1_100_000
        ),
    )(*far)
    return pl.pallas_call(
        place,
        out_shape=(tile, tile),
        in_specs=[vmem, vmem],
        out_specs=(hbm, hbm),
        scratch_shapes=[dma((2,))],
        compiler_params=pltpu.CompilerParams(vmem_limit_bytes=4 * 2**20),
        cost_estimate=pl.CostEstimate(flops=0, bytes_accessed=524288, transcendentals=0),
    )(update, mirrored)


def solution(mesh):
    placed = (P("row", "col", None), P(), P(), P(), P(), P(), P(), P())
    return jax.shard_map(
        per_device,
        mesh=mesh,
        in_specs=placed,
        out_specs=(P("row", "col", None), P("row", "col", None)),
        check_vma=False,
    )
```

```python
import jax
import jax.numpy as jnp
from jax import lax
from jax.experimental import pallas as pl
from jax.experimental.pallas import tpu as pltpu
from jax.sharding import PartitionSpec as P

EPSILON = 1e-05
MESH = pl.DeviceIdType.MESH
EARLY = 6
NT = (((1,), (1,)), ((), ()))


def dot(a, b):
    return jnp.dot(a, b, preferred_element_type=jnp.float32)


def div(a, b):
    return lax.div(a, jnp.int32(b))


def rem(a, b):
    return lax.rem(a, jnp.int32(b))


def outward(n, middle):
    return middle + div(n + 1, 2) * (1 - 2 * rem(n, 2))


def position(k):
    below = 1 - div(k, 4)
    return (1 - 2 * below) * 2 * (k - 4) - below


def dot_nt(a, b):
    return lax.dot_general(a, b, NT, preferred_element_type=jnp.float32)


def kernel(
    pair_hbm,
    gain_hbm,
    wq_hbm,
    wk_hbm,
    wv_hbm,
    wg_hbm,
    bw_hbm,
    wo_hbm,
    upd_ref,
    mir_ref,
    pair_ref,
    gain_ref,
    wq_ref,
    wk_ref,
    wv_ref,
    wg_ref,
    bw_ref,
    wo_ref,
    in_sem,
    nrm,
    xcat,
    wbd,
    b1buf,
    bbuf,
    biasf,
    xall,
    wkt,
    vbuf,
    scores,
    weights,
    inverse,
    gbuf,
    xq,
    ustage,
    ufull,
    mstage,
    mflat,
    s1_s,
    s1_r,
    s2_s,
    s2_r,
    b1_s,
    b1_r,
    b2_s,
    b2_r,
    b3_s,
    b3_r,
    o1_s,
    o1_r,
    o2_s,
    o2_r,
    m_s,
    m_r,
):
    r = lax.axis_index("row")
    c = lax.axis_index("col")
    x = div(r, 8)
    zh = rem(div(r, 2), 4)
    core = rem(r, 2)
    y = div(c, 2)
    zl = rem(c, 2)
    z = zh * 2 + zl
    sibling = (r + 1 - 2 * core, c)

    def col_peer(k):
        return (r, rem(c + k, 16))

    def x_row(xx):
        return xx * 8 + zh * 2 + core

    def y_peer(k):
        return (r, rem(y + k, 8) * 2 + zl)

    def z_peer(k):
        zz = rem(z + k, 8)
        return (x * 8 + div(zz, 2) * 2 + core, y * 2 + rem(zz, 2))

    def send(src, dst, s_sem, r_sem, dev):
        pltpu.make_async_remote_copy(
            src_ref=src,
            dst_ref=dst,
            send_sem=s_sem,
            recv_sem=r_sem,
            device_id=dev,
            device_id_type=MESH,
        ).start()

    def arrived(ref, sem):
        pltpu.make_async_copy(ref, ref, sem).wait()

    def loop(low, high, body):
        def step(k, carry):
            body(k)
            return carry

        lax.fori_loop(low, high, step, 0)

    loads = [
        pltpu.make_async_copy(src, dst, in_sem.at[i])
        for i, (src, dst) in enumerate(
            (
                (pair_hbm, pair_ref),
                (gain_hbm, gain_ref),
                (bw_hbm, bw_ref),
                (wk_hbm, wk_ref),
                (wv_hbm, wv_ref),
                (wq_hbm, wq_ref),
                (wg_hbm, wg_ref),
                (wo_hbm, wo_ref),
            )
        )
    ]
    for load in loads[:3]:
        load.start()

    barrier = pltpu.get_barrier_semaphore()

    def greet(dev):
        pl.semaphore_signal(barrier, inc=1, device_id=dev, device_id_type=MESH)

    loop(0, 15, lambda n: greet(col_peer(outward(n, 8))))
    loop(0, 7, lambda n: greet(z_peer(outward(n, 4))))
    loop(1, 4, lambda k: greet((x_row(rem(x + k, 4)), c)))
    greet(sibling)
    for load in loads[3:]:
        load.start()

    xcat[32:128] = jnp.zeros((96, 2048), jnp.bfloat16)
    heads = lax.broadcasted_iota(jnp.int32, (64, 4), 0) // 16
    pick = heads == lax.broadcasted_iota(jnp.int32, (64, 4), 1)
    row_j = lax.broadcasted_iota(jnp.int32, (64, 128), 0) % 16
    loads[2].wait()
    spread_w = dot(pick.astype(jnp.float32).astype(jnp.bfloat16), bw_ref[...])
    for j in range(16):
        wbd[:, j * 128 : (j + 1) * 128] = jnp.where(row_j == j, spread_w, 0.0).astype(
            jnp.bfloat16
        )

    loads[1].wait()
    loads[0].wait()
    entries = pair_ref[...].reshape(512, 128).astype(jnp.float32)
    center = jnp.mean(entries, axis=-1, keepdims=True)
    shifted = entries - center
    spread = jnp.mean(shifted * shifted, axis=-1, keepdims=True)
    gain = gain_ref[...].astype(jnp.float32)
    normed = (shifted * lax.rsqrt(spread + EPSILON) * gain).astype(jnp.bfloat16)
    nrm[...] = normed.reshape(16, 32, 128)

    for j in range(16):
        xcat[0:32, j * 128 : (j + 1) * 128] = nrm[j]
    by_head = dot_nt(wbd[...], xcat[...])
    packed = by_head[0:16]
    for h in range(1, 4):
        packed = packed + pltpu.roll(by_head[16 * h : 16 * h + 16], 32 * h, 1)
    b1buf[7] = packed.astype(jnp.bfloat16)

    pl.semaphore_wait(barrier, 26)

    def send_tile(n):
        k = outward(n, 4)
        send(b1buf.at[7], b1buf.at[n], b1_s, b1_r.at[n], y_peer(k))

    loop(0, 7, send_tile)
    def slot_rows(z_low, k):
        return pl.ds(pl.multiple_of((z_low * 8 + position(k)) * 32, 32), 32)

    def send_row(n):
        k = outward(14 - n, 8)
        col = rem(c + k, 16)
        send(
            nrm.at[col],
            xall.at[0, slot_rows(zl, rem(div(col, 2) - y + 8, 8))],
            s1_s,
            s1_r.at[k],
            (r, col),
        )

    loop(0, 15, send_row)
    xall[0, slot_rows(zl, jnp.int32(0))] = nrm[c]

    def share(col):
        rows = slot_rows(rem(col, 2), rem(y - div(col, 2) + 8, 8))
        piece = xall.at[0, rows]
        for d in (2, 1, 3):
            dev = (x_row(rem(x + d, 4)), c)
            send(piece, xall.at[d, rows], s2_s.at[d], s2_r.at[d], dev)

    def pass_row(n):
        k = outward(14 - n, 8)
        arrived(xall.at[0, pl.ds(0, 32)], s1_r.at[k])
        share(rem(c - k + 16, 16))

    share(c)
    lane_group = lax.broadcasted_iota(jnp.int32, (16, 128), 1) // 32

    def spread_bias(half, first, count):
        loop(first, first + count, lambda n: arrived(b1buf.at[0], b1_r.at[n]))
        tiles = [b1buf[4 * half + i].astype(jnp.float32) for i in range(4)]
        for h in range(4):
            merged = jnp.zeros((16, 128), jnp.float32)
            for i in range(4):
                turn = (i - h) * 32 % 128
                moved = pltpu.roll(tiles[i], turn, 1) if turn else tiles[i]
                merged = jnp.where(lane_group == i, moved, merged)
            bbuf[core, z, half, h * 16 : (h + 1) * 16] = merged.astype(jnp.bfloat16)
        block = bbuf.at[core, z, half]

        def send_bias(n):
            k = outward(n, 4)
            send(block, block, b2_s, b2_r.at[half * 8 + k], z_peer(k))

        loop(0, 7, send_bias)
        send(block, block, b3_s, b3_r.at[half * 8], sibling)

    spread_bias(1, 4, 3)
    loop(0, EARLY, pass_row)
    spread_bias(0, 0, 4)
    loop(EARLY, 15, pass_row)
    loads[3].wait()
    wkt[...] = wk_ref[...].astype(jnp.float32).T.astype(jnp.bfloat16)

    def project(d):
        keys = xall[d]
        kt = dot_nt(wkt[...], keys).astype(jnp.bfloat16)
        values = dot(keys, wv_ref[...])
        for h in range(4):
            vbuf[d, h * 512 : (h + 1) * 512] = jnp.where(
                head_of_key == h, values, 0.0
            ).astype(jnp.bfloat16)
        for q in range(4):
            k = rem(y - 2 * x - q // 2 + 8, 8)
            xq[q * 32 : (q + 1) * 32] = xall[d, slot_rows(q % 2, k)]
        own = xq[...]
        gbuf[d] = jax.nn.sigmoid(dot(own, wg_ref[...]))
        queries = (dot(own, wq_ref[...]) * 32**-0.5).astype(jnp.bfloat16)
        queries = queries.astype(jnp.float32)
        by_head = [
            jnp.where(head_of_lane == h, queries, 0.0).astype(jnp.bfloat16)
            for h in range(4)
        ]
        scores[d] = dot(jnp.concatenate(by_head, 0), kt)

    def lay_bias(side, zz, half):
        block = bbuf[side, zz, half].astype(jnp.float32)
        j0 = pl.multiple_of((div(zz, 2) * 2 + side) * 16, 16)
        lanes = slice(half * 128, half * 128 + 128)
        for h in range(4):
            biasf[rem(zz, 2), h, pl.ds(j0, 16), lanes] = block[h * 16 : (h + 1) * 16]

    head_of_lane = lax.broadcasted_iota(jnp.int32, (128, 128), 1) // 32
    head_of_key = lax.broadcasted_iota(jnp.int32, (512, 128), 1) // 32

    for load in loads[4:]:
        load.wait()

    def forward(half):
        def one(n):
            k = outward(6 - n, 4)
            zz = rem(z - k + 8, 8)
            block = bbuf.at[core, zz, half]
            arrived(block, b2_r.at[half * 8 + k])
            send(block, block, b3_s, b3_r.at[half * 8 + k], sibling)

        loop(0, 7, one)
        loop(1, 8, lambda k: lay_bias(core, rem(z + k, 8), half))

    def next_row(d):
        arrived(xall.at[d], s2_r.at[d])
        project(d)

    def take_bias(half):
        def one(n):
            k = outward(7 - n, 4)
            zz = rem(z - k + 8, 8)
            arrived(bbuf.at[0, 0, 0], b3_r.at[half * 8 + k])
            lay_bias(1 - core, zz, half)

        loop(0, 8, one)

    forward(1)
    lay_bias(core, z, 0)
    lay_bias(core, z, 1)
    project(0)
    forward(0)
    next_row(1)
    next_row(3)
    next_row(2)
    take_bias(1)
    take_bias(0)

    def weigh(d):
        scale = jnp.zeros((128, 128), jnp.float32)
        for h in range(4):
            bias = jnp.concatenate([biasf[0, h], biasf[1, h]], 1)
            logits = scores[d, h * 128 : (h + 1) * 128] + bias
            exponent = jnp.exp(logits - jnp.max(logits, axis=-1, keepdims=True))
            denominator = jnp.sum(exponent, axis=-1, keepdims=True)
            weights[d, :, h * 512 : (h + 1) * 512] = exponent.astype(jnp.bfloat16)
            scale = jnp.where(head_of_lane == h, 1.0 / denominator, scale)
        inverse[d] = scale

    def mix(d):
        attended = dot(weights[d], vbuf[d]) * inverse[d]
        gated = (gbuf[d] * attended).astype(jnp.bfloat16)
        ustage[d] = dot(gated, wo_ref[...]).astype(jnp.bfloat16)

    def mirror_copy(d, t):
        x_i = rem(x - d + 4, 4)
        to_row = x * 8 + t
        to_col = x_i * 4 + zh
        src = ustage.at[d, pl.ds(pl.multiple_of(t * 16, 16), 16)]
        dst = mstage.at[core * 16 + c]
        here = jnp.logical_and(to_row == r, to_col == c)
        return src, dst, (to_row, to_col), here

    def mirror_row(d, t):
        src, dst, dev, here = mirror_copy(d, t)

        @pl.when(here)
        def _():
            pltpu.make_async_copy(src, dst, m_r).start()

        @pl.when(jnp.logical_not(here))
        def _():
            send(src, dst, m_s, m_r, dev)

    def give(group):
        def one(q):
            cc = group * 4 + q
            src = ufull.at[group, pl.ds(pl.multiple_of(q * 32, 32), 32)]
            dst = upd_ref.at[c]

            @pl.when(cc == c)
            def _():
                pltpu.make_async_copy(src, dst, o2_r).start()

            @pl.when(cc != c)
            def _():
                send(src, dst, o2_s, o2_r, (r, cc))

        loop(0, 4, one)

    def emit(d):
        @pl.when(d > 0)
        def _():
            dev = (x_row(rem(x - d + 4, 4)), c)
            send(ustage.at[d], ufull.at[x], o1_s.at[d], o1_r.at[d], dev)

        loop(0, 4, lambda t: mirror_row(d, t))

        @pl.when(d == 0)
        def _():
            ufull[x] = ustage[0]
            give(x)

    far = rem(div(rem(y - div(zh, 2) + 8, 8) + 4, 2), 4)
    high = div(zh, 2)
    order = [
        d + high * (rem(x - rem(far + step, 4) + 4, 4) - d)
        for d, step in ((2, 0), (1, 1), (3, 3), (0, 2))
    ]
    for d in order:
        weigh(d)
        mix(d)
        emit(d)

    def pass_on(d):
        arrived(ufull.at[0], o1_r.at[d])
        give(rem(x + d, 4))

    pass_on(2)
    pass_on(1)
    pass_on(3)
    for d in order:
        loop(4, 8, lambda t: mirror_row(d, t))

    arrived(b1buf.at[pl.ds(0, 7)], b1_s)
    arrived(nrm.at[pl.ds(0, 15)], s1_s)
    arrived(bbuf.at[0, pl.ds(0, 7)], b2_s)
    arrived(bbuf.at[0], b3_s)
    loop(1, 4, lambda d: arrived(xall.at[0], s2_s.at[d]))
    loop(1, 4, lambda d: arrived(ustage.at[0], o1_s.at[d]))

    arrived(mstage, m_r)
    mflat[...] = mstage[...].astype(jnp.float32).reshape(512, 128)
    for j in range(16):
        mir_ref[j] = mflat[pl.ds(j, 32, stride=16), :].astype(jnp.bfloat16)

    stays = rem(c, 4) == zh

    @pl.when(stays)
    def _():
        arrived(mstage.at[pl.ds(0, 31)], m_s)

    @pl.when(jnp.logical_not(stays))
    def _():
        arrived(mstage, m_s)

    arrived(upd_ref.at[pl.ds(0, 15)], o2_s)
    arrived(upd_ref, o2_r)


def place(upd, mir, upd_out, mir_out, sem):
    writes = [
        pltpu.make_async_copy(upd, upd_out, sem.at[0]),
        pltpu.make_async_copy(mir, mir_out, sem.at[1]),
    ]
    for write in writes:
        write.start()
    for write in writes:
        write.wait()


def per_device(pair, gain, wq, wk, wv, wg, bw, wo):
    bf16, f32 = jnp.bfloat16, jnp.float32
    hbm = pl.BlockSpec(memory_space=pl.ANY)
    vmem = pl.BlockSpec(memory_space=pltpu.VMEM)
    near = pltpu.VMEM(pair.shape, bf16)
    dma = pltpu.SemaphoreType.DMA
    tile = jax.ShapeDtypeStruct(pair.shape, bf16)
    far = [
        pltpu.with_memory_space_constraint(array, pltpu.HBM)
        for array in (pair, gain.reshape(1, 128), wq, wk, wv, wg, bw.T, wo)
    ]
    update, mirrored = pl.pallas_call(
        kernel,
        out_shape=(near, near),
        in_specs=[hbm] * 8,
        out_specs=(vmem, vmem),
        scratch_shapes=[
            pltpu.VMEM((16, 32, 128), bf16),
            pltpu.VMEM((1, 128), bf16),
            pltpu.VMEM((128, 128), bf16),
            pltpu.VMEM((128, 128), bf16),
            pltpu.VMEM((128, 128), bf16),
            pltpu.VMEM((128, 128), bf16),
            pltpu.VMEM((4, 128), bf16),
            pltpu.VMEM((128, 128), bf16),
            dma((8,)),
            pltpu.VMEM((16, 32, 128), bf16),
            pltpu.VMEM((128, 2048), bf16),
            pltpu.VMEM((64, 2048), bf16),
            pltpu.VMEM((8, 16, 128), bf16),
            pltpu.VMEM((2, 8, 2, 64, 128), bf16),
            pltpu.VMEM((2, 4, 128, 256), f32),
            pltpu.VMEM((4, 512, 128), bf16),
            pltpu.VMEM((128, 128), bf16),
            pltpu.VMEM((4, 2048, 128), bf16),
            pltpu.VMEM((4, 512, 512), f32),
            pltpu.VMEM((4, 128, 2048), bf16),
            pltpu.VMEM((4, 128, 128), f32),
            pltpu.VMEM((4, 128, 128), f32),
            pltpu.VMEM((128, 128), bf16),
            pltpu.VMEM((4, 128, 128), bf16),
            pltpu.VMEM((4, 128, 128), bf16),
            pltpu.VMEM((32, 16, 128), bf16),
            pltpu.VMEM((512, 128), f32),
            dma,
            dma((16,)),
            dma((4,)),
            dma((4,)),
            dma,
            dma((8,)),
            dma,
            dma((16,)),
            dma,
            dma((16,)),
            dma((4,)),
            dma((4,)),
            dma,
            dma,
            dma,
            dma,
        ],
        compiler_params=pltpu.CompilerParams(
            collective_id=0, has_side_effects=True, vmem_limit_bytes=32 * 2**20
        ),
        cost_estimate=pl.CostEstimate(
            flops=1_000_000_000, bytes_accessed=1_000_000, transcendentals=1_100_000
        ),
    )(*far)
    return pl.pallas_call(
        place,
        out_shape=(tile, tile),
        in_specs=[vmem, vmem],
        out_specs=(hbm, hbm),
        scratch_shapes=[dma((2,))],
        compiler_params=pltpu.CompilerParams(vmem_limit_bytes=4 * 2**20),
        cost_estimate=pl.CostEstimate(flops=0, bytes_accessed=524288, transcendentals=0),
    )(update, mirrored)


def solution(mesh):
    placed = (P("row", "col", None), P(), P(), P(), P(), P(), P(), P())
    return jax.shard_map(
        per_device,
        mesh=mesh,
        in_specs=placed,
        out_specs=(P("row", "col", None), P("row", "col", None)),
        check_vma=False,
    )
```
